256 devices in a mesh: lat: 8 (over y, x_hi), lon: 32 (over z, x_lo, core).
Axes of the slice: x: 4 (x_hi: 2, x_lo: 2; x = x_hi * 2 + x_lo), y: 4, z: 8, core: 2. Of those that a mesh axis runs over, the one named last changes fastest.
Arguments:
- features: bfloat16 [4, 192, 384, 512], P(None, 'lat', 'lon'), may hold values from -6 to 6
- packed_first: bfloat16 [512, 1536], replicated, may hold values from -0.25 to 0.25
- scale_first: float32 [8], replicated, may hold values from 2 to 16
- output_first: bfloat16 [512, 512], replicated, may hold values from -0.25 to 0.25
- gain_first: float32 [512], replicated, may hold values from 0.5 to 1.5
- offset_first: float32 [512], replicated, may hold values from -1.5 to 1.5
- merge_weight: bfloat16 [2048, 1024], replicated, may hold values from -0.125 to 0.125
- merge_gain: float32 [1024], replicated, may hold values from 0.5 to 1.5
- merge_offset: float32 [1024], replicated, may hold values from -1.5 to 1.5
- packed_second: bfloat16 [1024, 1536], replicated, may hold values from -0.1875 to 0.1875
- scale_second: float32 [8], replicated, may hold values from 2 to 16
- output_second: bfloat16 [512, 1024], replicated, may hold values from -0.25 to 0.25
- gain_second: float32 [1024], replicated, may hold values from 0.5 to 1.5
- offset_second: float32 [1024], replicated, may hold values from -1.5 to 1.5
Outputs:
- coarse_out: bfloat16 [96, 32, 2, 12, 1024], P('lat', 'lon')
The draws below stay inside these ranges and needn't reach their ends.
All inputs are finite; a program needn't handle non-finite values.
Results may differ from the reference program's by a relative error of at most 0.019.
Values may be sent and summed in bfloat16 or wider, within the bound.
A program may use at most 128 MiB of HBM per device.

```python
import math
import jax
import jax.numpy as jnp
from jax import lax

LEVELS = 4
WLEV = 2
WLAT = 6
WLON = 12
HD = 64
HEADS1 = 8
HEADS2 = 8
D1 = 512
D2 = 1024
NLAT = 192
NLON = 384


def shard_levels(key, dims, shards, low, top_value):
    level, own = 1.0, jax.random.fold_in(key, 6)
    for axis_at, shards_of in shards:
        draws = jnp.exp(jax.random.uniform(jax.random.fold_in(own, axis_at), (shards_of,), jnp.float32, low / len(shards), top_value / len(shards)))
        level = level * jnp.repeat(draws, dims[axis_at] // shards_of).reshape([-1 if axis == axis_at else 1 for axis in range(len(dims))])
    return level


def gaussian(rng, dims, scale, bound, shards=(), dtype=jnp.bfloat16):
    values = jax.random.normal(rng, dims, jnp.float32) * scale
    if len(shards) > 0:
        values = shard_levels(rng, dims, shards, -0.22, 0.18) * values
    return jnp.clip(values, min=-bound, max=bound).astype(dtype)


def setup_inputs(seed: int = 0) -> dict:
    streams_of = jax.random.split(jax.random.key(seed), 15)
    return {
        "features": gaussian(streams_of[0], (LEVELS, NLAT, NLON, D1), 1.0, 6.0, ((1, 8), (2, 32))),
        "packed_first": gaussian(streams_of[1], (D1, 3 * HEADS1 * HD), D1 ** -0.5, 0.25),
        "scale_first": jnp.clip(jnp.exp(jax.random.uniform(streams_of[2], (HEADS1,), jnp.float32, math.log(2.0), math.log(16.0))), 2.0, 16.0),
        "output_first": gaussian(streams_of[3], (HEADS1 * HD, D1), (HEADS1 * HD) ** -0.5, 0.25),
        "gain_first": jnp.clip(1.0 + 0.1 * jax.random.normal(streams_of[4], (D1,), jnp.float32), 0.5, 1.5),
        "offset_first": gaussian(streams_of[5], (D1,), 0.3, 1.5, (), jnp.float32),
        "merge_weight": gaussian(streams_of[6], (4 * D1, D2), (4 * D1) ** -0.5, 0.125),
        "merge_gain": jnp.clip(1.0 + 0.1 * jax.random.normal(streams_of[7], (D2,), jnp.float32), 0.5, 1.5),
        "merge_offset": gaussian(streams_of[8], (D2,), 0.3, 1.5, (), jnp.float32),
        "packed_second": gaussian(streams_of[9], (D2, 3 * HEADS2 * HD), D2 ** -0.5, 0.1875),
        "scale_second": jnp.clip(jnp.exp(jax.random.uniform(streams_of[10], (HEADS2,), jnp.float32, math.log(2.0), math.log(16.0))), 2.0, 16.0),
        "output_second": gaussian(streams_of[11], (HEADS2 * HD, D2), (HEADS2 * HD) ** -0.5, 0.25),
        "gain_second": jnp.clip(1.0 + 0.1 * jax.random.normal(streams_of[12], (D2,), jnp.float32), 0.5, 1.5),
        "offset_second": gaussian(streams_of[13], (D2,), 0.3, 1.5, (), jnp.float32),
    }


norm_eps = 1e-05
unit_eps = 1e-06

def layer_norm(values, norm_gain, offset):
    average = lax.optimization_barrier(jnp.mean(values, axis=-1, keepdims=True))
    centred = values - average
    spread = lax.optimization_barrier(jnp.mean(centred * centred, axis=-1, keepdims=True))
    return centred * lax.rsqrt(spread + norm_eps) * norm_gain + offset

def unit_heads(tensor_in, head_count):
    shaped = tensor_in.astype(jnp.float32).reshape(tensor_in.shape[:-1] + (head_count, tensor_in.shape[-1] // head_count))
    scaled = shaped * lax.rsqrt(lax.optimization_barrier(jnp.sum(shaped * shaped, axis=-1, keepdims=True)) + unit_eps)
    return lax.optimization_barrier(scaled.astype(jnp.bfloat16)).astype(jnp.float32)

def attend(queries, keys_in, values_in, query_region, key_region, scales):
    head_count = scales.shape[0]
    query_unit = unit_heads(queries, head_count)
    key_unit = unit_heads(keys_in, head_count)
    scores = jnp.einsum('nahd,nbhd->nhab', query_unit, key_unit) * scales[None, :, None, None]
    allowed = (query_region[:, :, None] == key_region[:, None, :])[:, None]
    weights = jnp.where(allowed, jnp.exp(scores), jnp.zeros_like(scores))
    totals = lax.optimization_barrier(jnp.sum(weights, axis=-1))
    value_heads = values_in.astype(jnp.float32).reshape(values_in.shape[:-1] + (head_count, values_in.shape[-1] // head_count))
    rounded = lax.optimization_barrier(weights.astype(jnp.bfloat16)).astype(jnp.float32)
    mixture = jnp.einsum('nhab,nbhd->nahd', rounded, value_heads)
    mixture = mixture / jnp.transpose(totals, (0, 2, 1))[..., None]
    return mixture.reshape(queries.shape).astype(jnp.bfloat16)

def shifted_block(features, packed, scales, output_weight, norm_gain, offset):
    levels, row_count, col_count, channels = features.shape
    inner_width = packed.shape[1] // 3
    rolled = jnp.roll(features, (-(WLEV // 2), -(WLAT // 2), -(WLON // 2)), axis=(0, 1, 2))
    level_wrap = (jnp.arange(levels) >= levels - WLEV // 2).astype(jnp.int32)
    row_wrap = (jnp.arange(row_count) >= row_count - WLAT // 2).astype(jnp.int32)
    region = 2 * row_wrap[None, :] + level_wrap[:, None]
    region = jnp.broadcast_to(region[:, :, None], (levels, row_count, col_count))
    window_shape = (levels // WLEV, WLEV, row_count // WLAT, WLAT, col_count // WLON, WLON)
    axis_order = (2, 0, 4, 1, 3, 5)
    tokens = jnp.transpose(rolled.reshape(window_shape + (channels,)), axis_order + (6,))
    tokens = tokens.reshape(row_count // WLAT, levels // WLEV * (col_count // WLON), WLEV * WLAT * WLON, channels)
    regions = jnp.transpose(region.reshape(window_shape), axis_order).reshape(tokens.shape[:3])

    def one_band(pair_items):
        band_tokens, band_region = pair_items
        packed_rows = jnp.dot(band_tokens.reshape(-1, channels), packed, preferred_element_type=jnp.float32).astype(jnp.bfloat16)
        packed_rows = packed_rows.reshape(band_tokens.shape[0], band_tokens.shape[1], 3 * inner_width)
        context = attend(packed_rows[..., :inner_width], packed_rows[..., inner_width:2 * inner_width], packed_rows[..., 2 * inner_width:], band_region, band_region, scales)
        projected = jnp.dot(context.reshape(-1, inner_width), output_weight, preferred_element_type=jnp.float32)
        return layer_norm(projected, norm_gain, offset).reshape(band_tokens.shape[0], band_tokens.shape[1], -1)
    branch = lax.map(one_band, (tokens, regions))
    out_channels = branch.shape[-1]
    branch = branch.reshape((row_count // WLAT, levels // WLEV, col_count // WLON, WLEV, WLAT, WLON, out_channels))
    branch = jnp.transpose(branch, (1, 3, 0, 4, 2, 5, 6)).reshape(levels, row_count, col_count, out_channels)
    branch = jnp.roll(branch, (WLEV // 2, WLAT // 2, WLON // 2), axis=(0, 1, 2))
    return (features.astype(jnp.float32) + branch).astype(jnp.bfloat16)

def reference(features, packed_first, scale_first, output_first, gain_first, offset_first, merge_weight, merge_gain, merge_offset, packed_second, scale_second, output_second, gain_second, offset_second):
    first_out = shifted_block(features, packed_first, scale_first, output_first, gain_first, offset_first)
    levels, row_count, col_count, channels = first_out.shape
    merge_parts = first_out.reshape(levels, row_count // 2, 2, col_count // 2, 2, channels)
    merge_parts = jnp.transpose(merge_parts, (0, 1, 3, 4, 2, 5)).reshape(-1, 4 * channels)
    merged = layer_norm(jnp.dot(merge_parts, merge_weight, preferred_element_type=jnp.float32), merge_gain, merge_offset)
    merged = merged.astype(jnp.bfloat16).reshape(levels, row_count // 2, col_count // 2, -1)
    second = shifted_block(merged, packed_second, scale_second, output_second, gain_second, offset_second)
    wide_channels = second.shape[-1]
    blocks = col_count // 2 // WLON
    second = second.reshape(2, levels // 2, row_count // 2, blocks, WLON, wide_channels)
    second = jnp.transpose(second, (2, 3, 0, 1, 4, 5))
    return second.reshape(row_count // 2, 2 * blocks, levels // 2, WLON, wide_channels)
```

```python
import functools

import jax
import jax.numpy as jnp
import numpy as np
from jax import lax
from jax.experimental import pallas as pl
from jax.experimental.pallas import tpu as pltpu
from jax.sharding import PartitionSpec as P

ATOM = 40
CELLS = 36
WIN = 4 * ATOM
MESH = pl.DeviceIdType.MESH
BF16 = jnp.bfloat16
F32 = jnp.float32
LOG2E = 1.4426950408889634
NORM_EPS = 1e-05
UNIT_EPS = 1e-06


def level_of(p, j):
    return (2 * p + j + 1) % 4


@functools.lru_cache(None)
def tables():
    cut = np.zeros((160, 192), np.float32)
    for half in range(2):
        for p in range(2):
            for i in range(3):
                for j in range(2):
                    for c in range(6):
                        row = half * 80 + p * 40 + (i * 2 + j) * 6 + c
                        cut[row, (level_of(p, j) * 3 + i) * 16 + half * 6 + c] = 1
    pick = np.zeros((320, 320), np.float32)
    for cp in range(2):
        for rp in range(2):
            for p in range(2):
                for u in range(2):
                    for i in range(3):
                        for j in range(2):
                            for c in range(3):
                                row = (cp * 2 + rp) * 80 + p * 40 + u * 18 + (i * 2 + j) * 3 + c
                                fine = 6 * u + 2 * i + rp
                                col = fine // 3 * 80 + p * 40 + (fine % 3 * 2 + j) * 6 + 2 * c + cp
                                pick[row, col] = 1
    late = np.zeros((256, 160), np.float32)
    early = np.zeros((192, 160), np.float32)
    for half in range(2):
        for j in range(2):
            for u in range(2):
                for i in range(3):
                    for c in range(6):
                        src = (2 * half + c // 3) * 40 + u * 18 + (i * 2 + j) * 3 + c % 3
                        late[(u * 4 + half * 2 + j) * 32 + i * 6 + c, src] = 1
                        early[(half * 2 + j) * 48 + u * 18 + i * 6 + c, src] = 1
    place = np.zeros((192, 224), np.float32)
    for row in range(12):
        for col in range(12):
            half, c = (1, col) if col < 6 else (0, col - 6)
            if row < 3:
                src = 160 + half * 32 + row * 6 + c
            elif row < 9:
                src = half * 48 + (row - 3) * 6 + c
            else:
                src = 96 + half * 32 + (row - 9) * 6 + c
            place[row * 16 + col, src] = 1
    t = np.arange(WIN) % ATOM
    atom = np.arange(WIN) // ATOM
    keep = np.stack(
        [
            (t // 6 % 2)[:, None] == (t // 6 % 2)[None],
            (atom % 2)[:, None] == (atom % 2)[None],
            (t % 18 // 3 % 2)[:, None] == (t % 18 // 3 % 2)[None],
            (t < 18)[:, None] == (t < 18)[None],
        ]
    ).astype(np.float32)
    valid = np.broadcast_to((t < CELLS)[:, None], (WIN, 128)).astype(np.float32)
    group = np.arange(256) // 64
    heads = (group[:, None] == group[None]).astype(np.float32)
    b = lambda x: x.astype(jnp.bfloat16)
    return b(cut), b(pick), b(late), b(early), b(place), b(keep), valid, b(heads)


def layer_norm(values, gain, offset):
    average = jnp.mean(values, axis=-1, keepdims=True)
    centred = values - average
    spread = jnp.mean(centred * centred, axis=-1, keepdims=True)
    return centred * lax.rsqrt(spread + NORM_EPS) * gain + offset


def dot(a, b):
    return jnp.dot(a, b, preferred_element_type=F32)


def project(x, weight_ref, heads_ref, yn):
    for at in range(6):
        lanes = pl.ds(256 * at, 256)
        y = dot(x, weight_ref[:, lanes]).astype(BF16).astype(F32)
        if at < 4:
            y = y * lax.rsqrt(dot((y * y).astype(BF16), heads_ref[...]) + UNIT_EPS)
        yn[:, :, :, lanes] = y.reshape(4, 2, ATOM, 256)


def attend(yn, ctx, w, mask, valid_ref, scale_ref):
    low = lax.broadcasted_iota(jnp.int32, (WIN, 128), 1) < 64
    valid = valid_ref[...]
    zero = jnp.zeros_like(valid)
    for g in range(4):
        q = yn[:, w, :, pl.ds(128 * g, 128)].reshape(WIN, 128).astype(BF16)
        k = yn[:, w, :, pl.ds(512 + 128 * g, 128)].reshape(WIN, 128)
        v = yn[:, w, :, pl.ds(1024 + 128 * g, 128)].reshape(WIN, 128) * valid
        sides = []
        for side in range(2):
            mine = low if side == 0 else jnp.logical_not(low)
            key = jnp.where(mine, k, zero).astype(BF16)
            value = jnp.where(mine, v, valid).astype(BF16)
            score = lax.dot_general(q, key, (((1,), (1,)), ((), ())), preferred_element_type=F32)
            weight = jnp.exp2(score * (scale_ref[2 * g + side] * LOG2E)).astype(BF16) * mask
            sides.append(dot(weight, value))
        top = jnp.where(low, sides[0], sides[1])
        total = pltpu.roll(jnp.where(low, sides[1], sides[0]), 64, 1)
        ctx[:, w, :, pl.ds(128 * g, 128)] = (top / total).reshape(4, ATOM, 128)


def kernel(
    nlat, nlon,
    feat_hbm, packed1_hbm, out1_hbm, merge_hbm, packed2_hbm, out2_hbm,
    scale1, gain1, offset1, gainm, offsetm, scale2, gain2, offset2,
    cut, pick, late, early, place, keep, valid, heads,
    out,
    feat, packed1, wout1, wmerge, packed2, wout2,
    padded, send0, sendr, x, yn, ctx, first, picked, merged, mb, quarter, t0, t1, t2, r0, r1, r2,
    load_sem, s1, v1, s2, v2, s3, v3, s4, v4,
):
    lat, lon = lax.axis_index("lat"), lax.axis_index("lon")
    odd = lax.rem(lon, 2)
    even = odd == 0

    def peer(dlat, dlon):
        return (lax.rem(lat + dlat + nlat, nlat), lax.rem(lon + dlon + nlon, nlon))

    def send(src, dst, send_sem, recv_sem, where):
        return pltpu.make_async_remote_copy(
            src_ref=src, dst_ref=dst, send_sem=send_sem, recv_sem=recv_sem,
            device_id=where, device_id_type=MESH,
        )

    loads = [
        pltpu.make_async_copy(a, b, load_sem.at[n])
        for n, (a, b) in enumerate(
            [(feat_hbm, feat), (packed1_hbm, packed1), (out1_hbm, wout1),
             (merge_hbm, wmerge), (packed2_hbm, packed2), (out2_hbm, wout2)]
        )
    ]
    for load in loads:
        load.start()

    barrier = pltpu.get_barrier_semaphore()
    for dlat, dlon in [
        (0, 1), (0, -1), (0, -2), (1, 0), (1, 1), (-1, 0), (-1, -1), (-1, -2),
        (0, jnp.where(even, 2, -3)), (-1, jnp.where(even, 1, -3)),
    ]:
        pl.semaphore_signal(barrier, inc=1, device_id=peer(dlat, dlon), device_id_type=MESH)

    padded[...] = jnp.zeros_like(padded)
    loads[0].wait()
    for level in range(4):
        padded[level, :, 0:12, :] = feat[level]
    pl.semaphore_wait(barrier, jnp.where(even, 11, 9))

    feature_copies = [
        send(send0.at[pl.ds(2 * n + 1, 2)], x.at[1, pl.ds(2 * n, 2)], s1.at[n], v1.at[n], peer(0, -1))
        for n in range(3)
    ] + [
        send(send0.at[pl.ds(7, 1)], x.at[1, pl.ds(6, 1)], s1.at[3], v1.at[3], peer(0, -1)),
        send(send0.at[pl.ds(0, 1)], x.at[1, pl.ds(7, 1)], s1.at[4], v1.at[4], peer(-1, -1)),
        send(sendr, x.at[0, pl.ds(7, 1)], s1.at[5], v1.at[5], peer(-1, 0)),
    ]
    for n, hb in enumerate([1, 2, 3, 4, 5, 6, 7, 0]):
        tokens = padded[:, pl.ds(3 * hb, 3)].reshape(192, 512)
        atoms = dot(cut[...], tokens).astype(BF16)
        send0[hb] = atoms[:80]
        if hb > 0:
            x[0, hb - 1] = atoms[80:]
        else:
            sendr[0] = atoms[80:]
        if n in (1, 3, 5):
            feature_copies[n // 2].start()
        if n == 6:
            feature_copies[3].start()
    feature_copies[4].start()
    feature_copies[5].start()

    loads[1].wait()
    loads[2].wait()
    edge = send(first.at[:, pl.ds(0, 1)], first.at[:, pl.ds(8, 1)], s2, v2, peer(-1, 0))
    last_lat = lat == nlat - 1

    def band(b, carry):
        for n in range(3):
            @pl.when(b == n)
            def _():
                feature_copies[n].wait_recv()

        @pl.when(b == 3)
        def _():
            for n in range(3, 6):
                feature_copies[n].wait_recv()

        xb = x[:, pl.ds(2 * b, 2)].reshape(320, 512)
        project(xb, packed1, heads, yn)
        wrapped = jnp.where(jnp.logical_and(last_lat, b == 3), 1.0, 0.0).astype(F32)
        rows = keep[1].astype(F32) * wrapped + (1.0 - wrapped)
        attend(yn, ctx, 0, rows.astype(BF16), valid, scale1)
        attend(yn, ctx, 1, (rows * keep[0].astype(F32)).astype(BF16), valid, scale1)
        branch = layer_norm(
            dot(ctx[...].reshape(320, 512).astype(BF16), wout1[...]), gain1[...], offset1[...]
        )
        first[:, pl.ds(2 * b, 2)] = (xb.astype(F32) + branch).astype(BF16).reshape(2, 2, 80, 512)

        @pl.when(b == 0)
        def _():
            edge.start()
        return carry

    lax.fori_loop(0, 4, band, 0)

    edge.wait_recv()
    for half in range(2):
        for cb in range(2):
            fine = first[half, pl.ds(4 * cb + 1, 4)].reshape(320, 512)
            parts = dot(pick[...], fine).astype(BF16)
            for at in range(4):
                picked[pl.ds((half * 2 + cb) * 80, 80), pl.ds(512 * at, 512)] = parts[80 * at : 80 * at + 80]
    loads[3].wait()
    normed = layer_norm(dot(picked[...], wmerge[...]), gainm[...], offsetm[...])
    merged[...] = normed.reshape(2, 2, 2, ATOM, 1024)
    for half in range(2):
        for p in range(2):
            mb[half, p] = merged[half, :, p].reshape(80, 1024).astype(BF16)
    even_copies = [
        send(mb.at[0, 0], quarter.at[3], s3.at[0], v3.at[3], peer(0, -2)),
        send(mb.at[0, 1], quarter.at[3], s3.at[1], v3.at[3], peer(0, -1)),
        send(mb.at[1, 1], quarter.at[0], s3.at[2], v3.at[0], peer(0, 1)),
    ]
    odd_copies = [
        send(mb.at[0, 0], quarter.at[1], s3.at[0], v3.at[1], peer(0, -1)),
        send(mb.at[1, 0], quarter.at[2], s3.at[1], v3.at[2], peer(0, -1)),
    ]

    @pl.when(even)
    def _():
        for copy in even_copies:
            copy.start()
        quarter[0] = mb[1, 0]
        odd_copies[0].wait_recv()
        odd_copies[1].wait_recv()
        even_copies[0].wait_recv()

    @pl.when(jnp.logical_not(even))
    def _():
        for copy in odd_copies:
            copy.start()
        quarter[1] = mb[0, 1]
        quarter[2] = mb[1, 1]
        even_copies[2].wait_recv()
        even_copies[0].wait_recv()

    loads[4].wait()
    loads[5].wait()
    tokens = quarter[...]
    project(tokens.reshape(320, 1024), packed2, heads, yn)
    upper = odd.astype(F32)
    levels = keep[2].astype(F32) * upper + (1.0 - upper)
    final_copies = []
    for cb in (1, 0):
        if cb == 1:
            wrapped = jnp.where(last_lat, 1.0, 0.0).astype(F32)
            mask = levels * (keep[3].astype(F32) * wrapped + (1.0 - wrapped))
        else:
            mask = levels
        attend(yn, ctx, cb, mask.astype(BF16), valid, scale2)
        branch = layer_norm(
            dot(ctx[:, cb].reshape(WIN, 512).astype(BF16), wout2[...]), gain2[...], offset2[...]
        )
        own = quarter[...].astype(F32)[:, 40 * cb : 40 * cb + 40].reshape(WIN, 1024)
        second = (own + branch).astype(BF16)
        if cb == 1:
            units = dot(late[...], second).astype(BF16).reshape(2, 2, 2, 32, 1024)
            r1[0, 0] = units[0, 0, 0]
            t1[...] = units[0]
            t2[...] = units[1]
        else:
            units = dot(early[...], second).astype(BF16).reshape(2, 2, 48, 1024)
            r0[0, 0] = units[0, 0]
            t0[...] = units
        for half in range(2):
            for j in range(2):
                to = 2 * half + (0 if j == 0 else 1 - 2 * odd)
                n = half * 2 + j
                if cb == 1:
                    final_copies.append(
                        send(t2.at[half, j], r2.at[half, j], s4.at[n], v4.at[n], peer(1, to)))
                    final_copies[-1].start()
                if n > 0:
                    src, dst, base = (t1, r1, 3) if cb == 1 else (t0, r0, 6)
                    final_copies.append(
                        send(src.at[half, j], dst.at[half, j], s4.at[base + n], v4.at[base + n], peer(0, to)))
                    final_copies[-1].start()

    for copy in final_copies:
        copy.wait_recv()
    for level in range(2):
        j = 1 - level
        parts = [r[half, j] for r in (r0, r1, r2) for half in range(2)]
        rows = dot(place[...], jnp.concatenate(parts, axis=0))
        out[:, 0, level] = rows.astype(BF16).reshape(12, 16, 1024)[:, :12]

    for copy in feature_copies:
        copy.wait_send()
    edge.wait_send()

    @pl.when(even)
    def _():
        for copy in even_copies:
            copy.wait_send()

    @pl.when(jnp.logical_not(even))
    def _():
        for copy in odd_copies:
            copy.wait_send()

    for copy in final_copies:
        copy.wait_send()


def body(nlat, nlon, features, packed_first, scale_first, output_first, gain_first, offset_first,
         merge_weight, merge_gain, merge_offset,
         packed_second, scale_second, output_second, gain_second, offset_second):
    any_spec = pl.BlockSpec(memory_space=pl.ANY)
    vmem = pl.BlockSpec(memory_space=pltpu.VMEM)
    smem = pl.BlockSpec(memory_space=pltpu.SMEM)
    dma = pltpu.SemaphoreType.DMA
    row = lambda v: v.reshape(1, -1)
    return pl.pallas_call(
        functools.partial(kernel, nlat, nlon),
        out_shape=jax.ShapeDtypeStruct((12, 1, 2, 12, 1024), BF16),
        in_specs=[any_spec] * 6 + [smem] + [vmem] * 4 + [smem] + [vmem] * 2 + [vmem] * 8,
        out_specs=vmem,
        scratch_shapes=[
            pltpu.VMEM((4, 24, 12, 512), BF16),
            pltpu.VMEM((512, 1536), BF16),
            pltpu.VMEM((512, 512), BF16),
            pltpu.VMEM((2048, 1024), BF16),
            pltpu.VMEM((1024, 1536), BF16),
            pltpu.VMEM((512, 1024), BF16),
            pltpu.VMEM((4, 24, 16, 512), BF16),
            pltpu.VMEM((8, 80, 512), BF16),
            pltpu.VMEM((1, 80, 512), BF16),
            pltpu.VMEM((2, 8, 80, 512), BF16),
            pltpu.VMEM((4, 2, ATOM, 1536), F32),
            pltpu.VMEM((4, 2, ATOM, 512), F32),
            pltpu.VMEM((2, 9, 80, 512), BF16),
            pltpu.VMEM((320, 2048), BF16),
            pltpu.VMEM((2, 2, 2, ATOM, 1024), F32),
            pltpu.VMEM((2, 2, 80, 1024), BF16),
            pltpu.VMEM((4, 80, 1024), BF16),
            pltpu.VMEM((2, 2, 48, 1024), BF16),
            pltpu.VMEM((2, 2, 32, 1024), BF16),
            pltpu.VMEM((2, 2, 32, 1024), BF16),
            pltpu.VMEM((2, 2, 48, 1024), BF16),
            pltpu.VMEM((2, 2, 32, 1024), BF16),
            pltpu.VMEM((2, 2, 32, 1024), BF16),
            dma((6,)),
            dma((6,)), dma((6,)),
            dma, dma,
            dma((3,)), dma((4,)),
            dma((10,)), dma((10,)),
        ],
        compiler_params=pltpu.CompilerParams(
            collective_id=0, has_side_effects=True, vmem_limit_bytes=52 * 2**20
        ),
        cost_estimate=pl.CostEstimate(flops=6_000_000_000, bytes_accessed=14_000_000, transcendentals=2_000_000),
    )(
        features, packed_first, output_first, merge_weight, packed_second, output_second,
        scale_first, row(gain_first), row(offset_first), row(merge_gain), row(merge_offset),
        scale_second, row(gain_second), row(offset_second),
        *[jnp.asarray(t) for t in tables()],
    )


def solution(mesh):
    return jax.shard_map(
        functools.partial(body, mesh.shape["lat"], mesh.shape["lon"]),
        mesh=mesh,
        in_specs=(P(None, "lat", "lon", None),) + (P(),) * 13,
        out_specs=P("lat", "lon", None, None, None),
        check_vma=False,
    )
```

```python
import functools

import jax
import jax.numpy as jnp
import numpy as np
from jax import lax
from jax.experimental import pallas as pl
from jax.experimental.pallas import tpu as pltpu
from jax.sharding import PartitionSpec as P

ATOM = 40
CELLS = 36
WIN = 4 * ATOM
MESH = pl.DeviceIdType.MESH
BF16 = jnp.bfloat16
F32 = jnp.float32
LOG2E = 1.4426950408889634
NORM_EPS = 1e-05
UNIT_EPS = 1e-06


def level_of(p, j):
    return (2 * p + j + 1) % 4


@functools.lru_cache(None)
def tables():
    cut = np.zeros((2, 160, 192), np.float32)
    for part in range(2):
        for hb in range(4):
            for i in range(3):
                for j in range(2):
                    for c in range(6):
                        row = hb * 40 + (i * 2 + j) * 6 + c
                        cut[part, row, (j * 6 + c) * 16 + 3 * hb + i + 4 * part] = 1
    pick = np.zeros((320, 320), np.float32)
    for cp in range(2):
        for rp in range(2):
            for p in range(2):
                for u in range(2):
                    for i in range(3):
                        for j in range(2):
                            for c in range(3):
                                row = (cp * 2 + rp) * 80 + p * 40 + u * 18 + (i * 2 + j) * 3 + c
                                fine = 6 * u + 2 * i + rp
                                col = fine // 3 * 80 + p * 40 + (fine % 3 * 2 + j) * 6 + 2 * c + cp
                                pick[row, col] = 1
    late = np.zeros((640, 640), np.float32)
    early = np.zeros((576, 640), np.float32)
    for half in range(2):
        for j in range(2):
            for u in range(2):
                for i in range(3):
                    for c in range(6):
                        src = (2 * half + c // 3) * 40 + u * 18 + (i * 2 + j) * 3 + c % 3
                        for lane in range(4):
                            late[(u * 4 + half * 2 + j) * 80 + lane * 18 + i * 6 + c, lane * 160 + src] = 1
                            early[(half * 2 + j) * 144 + lane * 36 + u * 18 + i * 6 + c, lane * 160 + src] = 1
    place = np.zeros((4, 144, 608), np.float32)
    for lane in range(4):
        for row in range(12):
            for col in range(12):
                half, c = (1, col) if col < 6 else (0, col - 6)
                if row < 3:
                    src = 448 + 80 * half + lane * 18 + row * 6 + c
                elif row < 9:
                    src = 144 * half + lane * 36 + (row - 3) * 6 + c
                else:
                    src = 288 + 80 * half + lane * 18 + (row - 9) * 6 + c
                place[lane, row * 12 + col, src] = 1
    t = np.arange(WIN) % ATOM
    atom = np.arange(WIN) // ATOM
    keep = np.stack(
        [
            (t // 6 % 2)[:, None] == (t // 6 % 2)[None],
            (atom % 2)[:, None] == (atom % 2)[None],
            (t % 18 // 3 % 2)[:, None] == (t % 18 // 3 % 2)[None],
            (t < 18)[:, None] == (t < 18)[None],
        ]
    ).astype(np.float32)
    valid = np.broadcast_to((t < CELLS)[:, None], (WIN, 128)).astype(np.float32)
    group = np.arange(256) // 64
    heads = (group[:, None] == group[None]).astype(np.float32)
    b = lambda x: x.astype(jnp.bfloat16)
    return b(cut), b(pick), b(late), b(early), b(place), b(keep), valid, b(heads)


def layer_norm(values, gain, offset):
    average = jnp.mean(values, axis=-1, keepdims=True)
    centred = values - average
    spread = jnp.mean(centred * centred, axis=-1, keepdims=True)
    return centred * lax.rsqrt(spread + NORM_EPS) * gain + offset


def dot(a, b):
    return jnp.dot(a, b, preferred_element_type=F32)


def project(x, weight_ref, heads_ref, yn, start, count):
    for at in range(6):
        lanes = pl.ds(256 * at, 256)
        y = dot(x, weight_ref[:, lanes]).astype(BF16).astype(F32)
        if at < 4:
            y = y * lax.rsqrt(dot((y * y).astype(BF16), heads_ref[...]) + UNIT_EPS)
        yn[pl.ds(start, count), :, :, lanes] = y.reshape(count, 2, ATOM, 256)


def attend(yn, ctx, w, mask, valid_ref, scale_ref):
    low = lax.broadcasted_iota(jnp.int32, (WIN, 128), 1) < 64
    valid = valid_ref[...]
    zero = jnp.zeros_like(valid)
    for g in range(4):
        q = yn[:, w, :, pl.ds(128 * g, 128)].reshape(WIN, 128).astype(BF16)
        k = yn[:, w, :, pl.ds(512 + 128 * g, 128)].reshape(WIN, 128)
        v = yn[:, w, :, pl.ds(1024 + 128 * g, 128)].reshape(WIN, 128) * valid
        sides = []
        for side in range(2):
            mine = low if side == 0 else jnp.logical_not(low)
            key = jnp.where(mine, k, zero).astype(BF16)
            value = jnp.where(mine, v, valid).astype(BF16)
            score = lax.dot_general(q, key, (((1,), (1,)), ((), ())), preferred_element_type=F32)
            weight = jnp.exp2(score * (scale_ref[2 * g + side] * LOG2E)).astype(BF16) * mask
            sides.append(dot(weight, value))
        top = jnp.where(low, sides[0], sides[1])
        total = pltpu.roll(jnp.where(low, sides[1], sides[0]), 64, 1)
        ctx[:, w, :, pl.ds(128 * g, 128)] = (top / total).reshape(4, ATOM, 128)


def kernel(
    nlat, nlon,
    feat_hbm, packed1_hbm, out1_hbm, merge_hbm, packed2_hbm, out2_hbm,
    pick_hbm, late_hbm, early_hbm, place_hbm,
    scale1, gain1, offset1, gainm, offsetm, scale2, gain2, offset2,
    cut, keep, valid, heads,
    out,
    feat, packed1, wout1, wmerge, packed2, wout2, pick, late, early, place,
    send0, sendr, x, yn, ctx, first, picked, mb, quarter, t0, t1, t2, r0, r1, r2,
    load_sem, s1, v1, s2, v2, s3, v3, s4, v4,
):
    lat, lon = lax.axis_index("lat"), lax.axis_index("lon")
    odd = lax.rem(lon, 2)
    even = odd == 0

    def peer(dlat, dlon):
        return (lax.rem(lat + dlat + nlat, nlat), lax.rem(lon + dlon + nlon, nlon))

    def send(src, dst, send_sem, recv_sem, where):
        return pltpu.make_async_remote_copy(
            src_ref=src, dst_ref=dst, send_sem=send_sem, recv_sem=recv_sem,
            device_id=where, device_id_type=MESH,
        )

    loads = [
        pltpu.make_async_copy(a, b, load_sem.at[n])
        for n, (a, b) in enumerate(
            [(feat_hbm, feat), (packed1_hbm, packed1), (out1_hbm, wout1),
             (merge_hbm, wmerge), (packed2_hbm, packed2), (out2_hbm, wout2),
             (pick_hbm, pick), (late_hbm, late), (early_hbm, early), (place_hbm, place)]
        )
    ]
    for load in loads:
        load.start()

    barrier = pltpu.get_barrier_semaphore()
    for dlat, dlon in [
        (0, 1), (0, -1), (0, -2), (1, 0), (1, 1), (-1, 0), (-1, -1), (-1, -2),
        (0, jnp.where(even, 2, -3)), (-1, jnp.where(even, 1, -3)),
    ]:
        pl.semaphore_signal(barrier, inc=1, device_id=peer(dlat, dlon), device_id_type=MESH)

    loads[0].wait()
    pl.semaphore_wait(barrier, jnp.where(even, 11, 9))

    feature_copies = [
        send(send0.at[pl.ds(2 * n + 1, 2)], x.at[1, pl.ds(2 * n, 2)], s1.at[n], v1.at[n], peer(0, -1))
        for n in range(3)
    ] + [
        send(send0.at[pl.ds(7, 1)], x.at[1, pl.ds(6, 1)], s1.at[3], v1.at[3], peer(0, -1)),
        send(send0.at[pl.ds(0, 1)], x.at[1, pl.ds(7, 1)], s1.at[4], v1.at[4], peer(-1, -1)),
        send(sendr, x.at[0, pl.ds(7, 1)], s1.at[5], v1.at[5], peer(-1, 0)),
    ]
    for half in range(2):
        for part in range(2):
            pair = []
            for p in range(2):
                tokens = jnp.stack([
                    feat[level_of(p, j), 6 * half : 6 * half + 6].astype(F32)[:, 8 * part : 8 * part + 16]
                    for j in range(2)
                ]).astype(BF16).reshape(192, 512)
                pair.append(dot(cut[part], tokens).reshape(4, ATOM, 512))
            atoms = jnp.concatenate(pair, axis=1).astype(BF16)
            if half == 0:
                send0[pl.ds(4 * part, 4)] = atoms
                if part == 0:
                    feature_copies[0].start()
                else:
                    for copy in feature_copies[1:5]:
                        copy.start()
            elif part == 0:
                sendr[...] = atoms[:1]
                feature_copies[5].start()
                x[0, pl.ds(0, 3)] = atoms[1:]
            else:
                x[0, pl.ds(3, 4)] = atoms

    loads[1].wait()
    loads[2].wait()
    edge = send(first.at[:, pl.ds(0, 1)], first.at[:, pl.ds(8, 1)], s2, v2, peer(-1, 0))
    last_lat = lat == nlat - 1

    def band(b, carry):
        for n in range(3):
            @pl.when(b == n)
            def _():
                feature_copies[n].wait_recv()

        @pl.when(b == 3)
        def _():
            for n in range(3, 6):
                feature_copies[n].wait_recv()

        xb = x[:, pl.ds(2 * b, 2)].reshape(320, 512)
        project(xb, packed1, heads, yn, 0, 4)
        wrapped = jnp.where(jnp.logical_and(last_lat, b == 3), 1.0, 0.0).astype(F32)
        rows = keep[1].astype(F32) * wrapped + (1.0 - wrapped)
        attend(yn, ctx, 0, rows.astype(BF16), valid, scale1)
        attend(yn, ctx, 1, (rows * keep[0].astype(F32)).astype(BF16), valid, scale1)
        branch = layer_norm(
            dot(ctx[...].reshape(320, 512).astype(BF16), wout1[...]), gain1[...], offset1[...]
        )
        first[:, pl.ds(2 * b, 2)] = (xb.astype(F32) + branch).astype(BF16).reshape(2, 2, 80, 512)

        @pl.when(b == 0)
        def _():
            edge.start()
        return carry

    lax.fori_loop(0, 4, band, 0)

    even_copies = [
        send(mb.at[0, 0], quarter.at[3], s3.at[0], v3.at[3], peer(0, -2)),
        send(mb.at[0, 1], quarter.at[3], s3.at[1], v3.at[3], peer(0, -1)),
        send(mb.at[1, 1], quarter.at[0], s3.at[2], v3.at[0], peer(0, 1)),
    ]
    odd_copies = [
        send(mb.at[0, 0], quarter.at[1], s3.at[0], v3.at[1], peer(0, -1)),
        send(mb.at[1, 0], quarter.at[2], s3.at[1], v3.at[2], peer(0, -1)),
    ]
    edge.wait_recv()
    loads[6].wait()
    loads[3].wait()
    for half in range(2):
        for cb in range(2):
            fine = first[half, pl.ds(4 * cb + 1, 4)].reshape(320, 512)
            parts = dot(pick[...], fine).astype(BF16)
            for at in range(4):
                picked[half, pl.ds(cb * 80, 80), pl.ds(512 * at, 512)] = parts[80 * at : 80 * at + 80]
        normed = layer_norm(dot(picked[half], wmerge[...]), gainm[...], offsetm[...])
        pairs = normed.reshape(2, 2, ATOM, 1024)
        for p in range(2):
            mb[half, p] = pairs[:, p].reshape(80, 1024).astype(BF16)

        @pl.when(even)
        def _():
            if half == 0:
                even_copies[0].start()
                even_copies[1].start()
            else:
                even_copies[2].start()
                quarter[0] = mb[1, 0]
                odd_copies[0].wait_recv()
                odd_copies[1].wait_recv()

        @pl.when(jnp.logical_not(even))
        def _():
            odd_copies[half].start()
            quarter[1 + half] = mb[half, 1]
            if half == 1:
                even_copies[2].wait_recv()

    loads[4].wait()
    loads[5].wait()
    project(quarter[pl.ds(0, 3)].reshape(240, 1024), packed2, heads, yn, 0, 3)
    even_copies[0].wait_recv()
    project(quarter[3], packed2, heads, yn, 3, 1)
    for load in loads[7:]:
        load.wait()
    upper = odd.astype(F32)
    levels = keep[2].astype(F32) * upper + (1.0 - upper)
    final_copies = []
    for cb in (1, 0):
        if cb == 1:
            wrapped = jnp.where(last_lat, 1.0, 0.0).astype(F32)
            mask = levels * (keep[3].astype(F32) * wrapped + (1.0 - wrapped))
        else:
            mask = levels
        attend(yn, ctx, cb, mask.astype(BF16), valid, scale2)
        branch = layer_norm(
            dot(ctx[:, cb].reshape(WIN, 512).astype(BF16), wout2[...]), gain2[...], offset2[...]
        )
        own = quarter[...].astype(F32)[:, 40 * cb : 40 * cb + 40].reshape(WIN, 1024)
        second = (own + branch).astype(BF16)
        stacked = jnp.concatenate([second[:, 256 * n : 256 * n + 256] for n in range(4)], axis=0)
        if cb == 1:
            units = dot(late[...], stacked).astype(BF16).reshape(2, 2, 2, 80, 256)
            r1[0, 0] = units[0, 0, 0]
            t1[...] = units[0]
            t2[...] = units[1]
        else:
            units = dot(early[...], stacked).astype(BF16).reshape(2, 2, 144, 256)
            r0[0, 0] = units[0, 0]
            t0[...] = units
        for half in range(2):
            for j in range(2):
                to = 2 * half + (0 if j == 0 else 1 - 2 * odd)
                n = half * 2 + j
                if cb == 1:
                    final_copies.append(
                        send(t2.at[half, j], r2.at[half, j], s4.at[n], v4.at[n], peer(1, to)))
                    final_copies[-1].start()
                if n > 0:
                    src, dst, base = (t1, r1, 3) if cb == 1 else (t0, r0, 6)
                    final_copies.append(
                        send(src.at[half, j], dst.at[half, j], s4.at[base + n], v4.at[base + n], peer(0, to)))
                    final_copies[-1].start()

    for copy in final_copies:
        copy.wait_recv()
    for level in range(2):
        j = 1 - level
        parts = [r[half, j] for r in (r0, r1, r2) for half in range(2)]
        parts = jnp.concatenate(parts, axis=0)
        for n in range(4):
            out[level, :, pl.ds(256 * n, 256)] = dot(place[n], parts).astype(BF16)

    for copy in feature_copies:
        copy.wait_send()
    edge.wait_send()

    @pl.when(even)
    def _():
        for copy in even_copies:
            copy.wait_send()

    @pl.when(jnp.logical_not(even))
    def _():
        for copy in odd_copies:
            copy.wait_send()

    for copy in final_copies:
        copy.wait_send()


def body(nlat, nlon, features, packed_first, scale_first, output_first, gain_first, offset_first,
         merge_weight, merge_gain, merge_offset,
         packed_second, scale_second, output_second, gain_second, offset_second):
    any_spec = pl.BlockSpec(memory_space=pl.ANY)
    vmem = pl.BlockSpec(memory_space=pltpu.VMEM)
    smem = pl.BlockSpec(memory_space=pltpu.SMEM)
    dma = pltpu.SemaphoreType.DMA
    row = lambda v: v.reshape(1, -1)
    *small, keep, valid, heads = [jnp.asarray(t) for t in tables()]
    cut, pick, late, early, place = small
    out = pl.pallas_call(
        functools.partial(kernel, nlat, nlon),
        out_shape=jax.ShapeDtypeStruct((2, 144, 1024), BF16),
        in_specs=[any_spec] * 10 + [smem] + [vmem] * 4 + [smem] + [vmem] * 2 + [vmem] * 4,
        out_specs=vmem,
        scratch_shapes=[
            pltpu.VMEM((4, 12, 24, 512), BF16),
            pltpu.VMEM((512, 1536), BF16),
            pltpu.VMEM((512, 512), BF16),
            pltpu.VMEM((2048, 1024), BF16),
            pltpu.VMEM((1024, 1536), BF16),
            pltpu.VMEM((512, 1024), BF16),
            pltpu.VMEM((320, 320), BF16),
            pltpu.VMEM((640, 640), BF16),
            pltpu.VMEM((576, 640), BF16),
            pltpu.VMEM((4, 144, 608), BF16),
            pltpu.VMEM((8, 80, 512), BF16),
            pltpu.VMEM((1, 80, 512), BF16),
            pltpu.VMEM((2, 8, 80, 512), BF16),
            pltpu.VMEM((4, 2, ATOM, 1536), F32),
            pltpu.VMEM((4, 2, ATOM, 512), F32),
            pltpu.VMEM((2, 9, 80, 512), BF16),
            pltpu.VMEM((2, 160, 2048), BF16),
            pltpu.VMEM((2, 2, 80, 1024), BF16),
            pltpu.VMEM((4, 80, 1024), BF16),
            pltpu.VMEM((2, 2, 144, 256), BF16),
            pltpu.VMEM((2, 2, 80, 256), BF16),
            pltpu.VMEM((2, 2, 80, 256), BF16),
            pltpu.VMEM((2, 2, 144, 256), BF16),
            pltpu.VMEM((2, 2, 80, 256), BF16),
            pltpu.VMEM((2, 2, 80, 256), BF16),
            dma((10,)),
            dma((6,)), dma((6,)),
            dma, dma,
            dma((3,)), dma((4,)),
            dma((10,)), dma((10,)),
        ],
        compiler_params=pltpu.CompilerParams(
            collective_id=0, has_side_effects=True, vmem_limit_bytes=52 * 2**20
        ),
        cost_estimate=pl.CostEstimate(flops=6_000_000_000, bytes_accessed=14_000_000, transcendentals=2_000_000),
    )(
        jnp.transpose(features, (0, 2, 1, 3)), packed_first, output_first, merge_weight, packed_second, output_second,
        pick, late, early, place,
        scale_first, row(gain_first), row(offset_first), row(merge_gain), row(merge_offset),
        scale_second, row(gain_second), row(offset_second),
        cut, keep, valid, heads,
    )
    return jnp.transpose(out.reshape(2, 12, 1, 12, 1024), (1, 2, 0, 3, 4))


def solution(mesh):
    return jax.shard_map(
        functools.partial(body, mesh.shape["lat"], mesh.shape["lon"]),
        mesh=mesh,
        in_specs=(P(None, "lat", "lon", None),) + (P(),) * 13,
        out_specs=P("lat", "lon", None, None, None),
        check_vma=False,
    )
```

```python
import functools

import jax
import jax.numpy as jnp
import numpy as np
from jax import lax
from jax.experimental import pallas as pl
from jax.experimental.pallas import tpu as pltpu
from jax.sharding import PartitionSpec as P

ATOM = 40
CELLS = 36
WIN = 4 * ATOM
MESH = pl.DeviceIdType.MESH
BF16 = jnp.bfloat16
F32 = jnp.float32
LOG2E = 1.4426950408889634
NORM_EPS = 1e-05
UNIT_EPS = 1e-06


def level_of(p, j):
    return (2 * p + j + 1) % 4


@functools.lru_cache(None)
def tables():
    cut = np.zeros((2, 160, 192), np.float32)
    for part in range(2):
        for hb in range(4):
            for i in range(3):
                for j in range(2):
                    for c in range(6):
                        row = hb * 40 + (i * 2 + j) * 6 + c
                        cut[part, row, (j * 6 + c) * 16 + 3 * hb + i + 4 * part] = 1
    pick = np.zeros((320, 320), np.float32)
    for cp in range(2):
        for rp in range(2):
            for p in range(2):
                for u in range(2):
                    for i in range(3):
                        for j in range(2):
                            for c in range(3):
                                row = (cp * 2 + rp) * 80 + p * 40 + u * 18 + (i * 2 + j) * 3 + c
                                fine = 6 * u + 2 * i + rp
                                col = fine // 3 * 80 + p * 40 + (fine % 3 * 2 + j) * 6 + 2 * c + cp
                                pick[row, col] = 1
    late = np.zeros((640, 640), np.float32)
    early = np.zeros((576, 640), np.float32)
    for half in range(2):
        for j in range(2):
            for u in range(2):
                for i in range(3):
                    for c in range(6):
                        src = (2 * half + c // 3) * 40 + u * 18 + (i * 2 + j) * 3 + c % 3
                        for lane in range(4):
                            late[(u * 4 + half * 2 + j) * 80 + lane * 18 + i * 6 + c, lane * 160 + src] = 1
                            early[(half * 2 + j) * 144 + lane * 36 + u * 18 + i * 6 + c, lane * 160 + src] = 1
    place = np.zeros((4, 144, 608), np.float32)
    for lane in range(4):
        for row in range(12):
            for col in range(12):
                half, c = (1, col) if col < 6 else (0, col - 6)
                if row < 3:
                    src = 448 + 80 * half + lane * 18 + row * 6 + c
                elif row < 9:
                    src = 144 * half + lane * 36 + (row - 3) * 6 + c
                else:
                    src = 288 + 80 * half + lane * 18 + (row - 9) * 6 + c
                place[lane, row * 12 + col, src] = 1
    t = np.arange(WIN) % ATOM
    atom = np.arange(WIN) // ATOM
    keep = np.stack(
        [
            (t // 6 % 2)[:, None] == (t // 6 % 2)[None],
            (atom % 2)[:, None] == (atom % 2)[None],
            (t % 18 // 3 % 2)[:, None] == (t % 18 // 3 % 2)[None],
            (t < 18)[:, None] == (t < 18)[None],
        ]
    ).astype(np.float32)
    valid = np.broadcast_to((t < CELLS)[:, None], (WIN, 128)).astype(np.float32)
    group = np.arange(256) // 64
    heads = (group[:, None] == group[None]).astype(np.float32)
    b = lambda x: x.astype(jnp.bfloat16)
    return b(cut), b(pick), b(late), b(early), b(place), b(keep), valid, b(heads)


def layer_norm(values, gain, offset):
    average = jnp.mean(values, axis=-1, keepdims=True)
    centred = values - average
    spread = jnp.mean(centred * centred, axis=-1, keepdims=True)
    return centred * lax.rsqrt(spread + NORM_EPS) * gain + offset


def dot(a, b):
    return jnp.dot(a, b, preferred_element_type=F32)


def project(x, weight_ref, heads_ref, yn, start, count):
    for at in range(6):
        lanes = pl.ds(256 * at, 256)
        y = dot(x, weight_ref[:, lanes]).astype(BF16).astype(F32)
        if at < 4:
            y = y * lax.rsqrt(dot((y * y).astype(BF16), heads_ref[...]) + UNIT_EPS)
        yn[pl.ds(start, count), :, :, lanes] = y.reshape(count, 2, ATOM, 256)


def attend(yn, ctx, w, mask, valid_ref, scale_ref):
    low = lax.broadcasted_iota(jnp.int32, (WIN, 128), 1) < 64
    valid = valid_ref[...]
    zero = jnp.zeros_like(valid)
    for g in range(4):
        q = yn[:, w, :, pl.ds(128 * g, 128)].reshape(WIN, 128).astype(BF16)
        k = yn[:, w, :, pl.ds(512 + 128 * g, 128)].reshape(WIN, 128)
        v = yn[:, w, :, pl.ds(1024 + 128 * g, 128)].reshape(WIN, 128) * valid
        sides = []
        for side in range(2):
            mine = low if side == 0 else jnp.logical_not(low)
            key = jnp.where(mine, k, zero).astype(BF16)
            value = jnp.where(mine, v, valid).astype(BF16)
            score = lax.dot_general(q, key, (((1,), (1,)), ((), ())), preferred_element_type=F32)
            weight = jnp.exp2(score * (scale_ref[2 * g + side] * LOG2E)).astype(BF16) * mask
            sides.append(dot(weight, value))
        top = jnp.where(low, sides[0], sides[1])
        total = pltpu.roll(jnp.where(low, sides[1], sides[0]), 64, 1)
        ctx[:, w, :, pl.ds(128 * g, 128)] = (top / total).reshape(4, ATOM, 128)


def kernel(
    nlat, nlon,
    feat_hbm, packed1_hbm, out1_hbm, merge_hbm, packed2_hbm, out2_hbm,
    pick_hbm, late_hbm, early_hbm, place_hbm,
    scale1_hbm, gain1_hbm, offset1_hbm, gainm_hbm, offsetm_hbm, scale2_hbm, gain2_hbm, offset2_hbm,
    cut_hbm, keep_hbm, valid_hbm, heads_hbm,
    out,
    feat, packed1, wout1, wmerge, packed2, wout2, pick, late, early, place,
    scale1, gain1, offset1, gainm, offsetm, scale2, gain2, offset2, cut, keep, valid, heads,
    send0, sendr, x, yn, ctx, first, picked, mb, quarter, t0, t1, t2, r0, r1, r2,
    load_sem, s1, v1, s2, v2, s3, v3, s4, v4,
):
    lat, lon = lax.axis_index("lat"), lax.axis_index("lon")
    odd = lax.rem(lon, 2)
    even = odd == 0

    def peer(dlat, dlon):
        return (lax.rem(lat + dlat + nlat, nlat), lax.rem(lon + dlon + nlon, nlon))

    def send(src, dst, send_sem, recv_sem, where):
        return pltpu.make_async_remote_copy(
            src_ref=src, dst_ref=dst, send_sem=send_sem, recv_sem=recv_sem,
            device_id=where, device_id_type=MESH,
        )

    def load(*pairs):
        copies = [pltpu.make_async_copy(a, b, load_sem.at[order.pop()]) for a, b in pairs]
        for copy in copies:
            copy.start()

        def wait():
            for copy in copies:
                copy.wait()

        return wait

    order = list(range(22))
    cut_loaded = load((feat_hbm, feat), (cut_hbm, cut))
    first_loaded = load(
        (packed1_hbm, packed1), (heads_hbm, heads), (keep_hbm, keep), (valid_hbm, valid), (scale1_hbm, scale1),
        (out1_hbm, wout1), (gain1_hbm, gain1), (offset1_hbm, offset1),
    )
    merge_loaded = load((pick_hbm, pick), (merge_hbm, wmerge), (gainm_hbm, gainm), (offsetm_hbm, offsetm))
    second_loaded = load(
        (packed2_hbm, packed2), (out2_hbm, wout2), (scale2_hbm, scale2), (gain2_hbm, gain2), (offset2_hbm, offset2),
        (late_hbm, late), (early_hbm, early), (place_hbm, place),
    )

    barrier = pltpu.get_barrier_semaphore()
    for dlat, dlon in [
        (0, 1), (0, -1), (0, -2), (1, 0), (1, 1), (-1, 0), (-1, -1), (-1, -2),
        (0, jnp.where(even, 2, -3)), (-1, jnp.where(even, 1, -3)),
    ]:
        pl.semaphore_signal(barrier, inc=1, device_id=peer(dlat, dlon), device_id_type=MESH)

    cut_loaded()
    pl.semaphore_wait(barrier, jnp.where(even, 11, 9))

    feature_copies = [
        send(send0.at[pl.ds(2 * n + 1, 2)], x.at[1, pl.ds(2 * n, 2)], s1.at[n], v1.at[n], peer(0, -1))
        for n in range(3)
    ] + [
        send(send0.at[pl.ds(7, 1)], x.at[1, pl.ds(6, 1)], s1.at[3], v1.at[3], peer(0, -1)),
        send(send0.at[pl.ds(0, 1)], x.at[1, pl.ds(7, 1)], s1.at[4], v1.at[4], peer(-1, -1)),
        send(sendr, x.at[0, pl.ds(7, 1)], s1.at[5], v1.at[5], peer(-1, 0)),
    ]
    for half in range(2):
        for part in range(2):
            pair = []
            for p in range(2):
                tokens = jnp.stack([
                    feat[level_of(p, j), 6 * half : 6 * half + 6].astype(F32)[:, 8 * part : 8 * part + 16]
                    for j in range(2)
                ]).astype(BF16).reshape(192, 512)
                pair.append(dot(cut[part], tokens).reshape(4, ATOM, 512))
            atoms = jnp.concatenate(pair, axis=1).astype(BF16)
            if half == 0:
                send0[pl.ds(4 * part, 4)] = atoms
                if part == 0:
                    feature_copies[0].start()
                else:
                    for copy in feature_copies[1:5]:
                        copy.start()
            elif part == 0:
                sendr[...] = atoms[:1]
                feature_copies[5].start()
                x[0, pl.ds(0, 3)] = atoms[1:]
            else:
                x[0, pl.ds(3, 4)] = atoms

    first_loaded()
    edge = send(first.at[:, pl.ds(0, 1)], first.at[:, pl.ds(8, 1)], s2, v2, peer(-1, 0))
    last_lat = lat == nlat - 1

    def band(b, carry):
        for n in range(3):
            @pl.when(b == n)
            def _():
                feature_copies[n].wait_recv()

        @pl.when(b == 3)
        def _():
            for n in range(3, 6):
                feature_copies[n].wait_recv()

        xb = x[:, pl.ds(2 * b, 2)].reshape(320, 512)
        project(xb, packed1, heads, yn, 0, 4)
        wrapped = jnp.where(jnp.logical_and(last_lat, b == 3), 1.0, 0.0).astype(F32)
        rows = keep[1].astype(F32) * wrapped + (1.0 - wrapped)
        attend(yn, ctx, 0, rows.astype(BF16), valid, scale1)
        attend(yn, ctx, 1, (rows * keep[0].astype(F32)).astype(BF16), valid, scale1)
        branch = layer_norm(
            dot(ctx[...].reshape(320, 512).astype(BF16), wout1[...]), gain1[...], offset1[...]
        )
        first[:, pl.ds(2 * b, 2)] = (xb.astype(F32) + branch).astype(BF16).reshape(2, 2, 80, 512)

        @pl.when(b == 0)
        def _():
            edge.start()
        return carry

    lax.fori_loop(0, 4, band, 0)

    even_copies = [
        send(mb.at[0, 0], quarter.at[3], s3.at[0], v3.at[3], peer(0, -2)),
        send(mb.at[0, 1], quarter.at[3], s3.at[1], v3.at[3], peer(0, -1)),
        send(mb.at[1, 1], quarter.at[0], s3.at[2], v3.at[0], peer(0, 1)),
    ]
    odd_copies = [
        send(mb.at[0, 0], quarter.at[1], s3.at[0], v3.at[1], peer(0, -1)),
        send(mb.at[1, 0], quarter.at[2], s3.at[1], v3.at[2], peer(0, -1)),
    ]
    edge.wait_recv()
    merge_loaded()
    for half in range(2):
        for cb in range(2):
            fine = first[half, pl.ds(4 * cb + 1, 4)].reshape(320, 512)
            parts = dot(pick[...], fine).astype(BF16)
            for at in range(4):
                picked[half, pl.ds(cb * 80, 80), pl.ds(512 * at, 512)] = parts[80 * at : 80 * at + 80]
        normed = layer_norm(dot(picked[half], wmerge[...]), gainm[...], offsetm[...])
        pairs = normed.reshape(2, 2, ATOM, 1024)
        for p in range(2):
            mb[half, p] = pairs[:, p].reshape(80, 1024).astype(BF16)

        @pl.when(even)
        def _():
            if half == 0:
                even_copies[0].start()
                even_copies[1].start()
            else:
                even_copies[2].start()
                quarter[0] = mb[1, 0]
                odd_copies[0].wait_recv()
                odd_copies[1].wait_recv()

        @pl.when(jnp.logical_not(even))
        def _():
            odd_copies[half].start()
            quarter[1 + half] = mb[half, 1]
            if half == 1:
                even_copies[2].wait_recv()

    second_loaded()
    project(quarter[pl.ds(0, 3)].reshape(240, 1024), packed2, heads, yn, 0, 3)
    even_copies[0].wait_recv()
    project(quarter[3], packed2, heads, yn, 3, 1)
    upper = odd.astype(F32)
    levels = keep[2].astype(F32) * upper + (1.0 - upper)
    final_copies = []
    for cb in (1, 0):
        if cb == 1:
            wrapped = jnp.where(last_lat, 1.0, 0.0).astype(F32)
            mask = levels * (keep[3].astype(F32) * wrapped + (1.0 - wrapped))
        else:
            mask = levels
        attend(yn, ctx, cb, mask.astype(BF16), valid, scale2)
        branch = layer_norm(
            dot(ctx[:, cb].reshape(WIN, 512).astype(BF16), wout2[...]), gain2[...], offset2[...]
        )
        own = quarter[...].astype(F32)[:, 40 * cb : 40 * cb + 40].reshape(WIN, 1024)
        second = (own + branch).astype(BF16)
        stacked = jnp.concatenate([second[:, 256 * n : 256 * n + 256] for n in range(4)], axis=0)
        if cb == 1:
            units = dot(late[...], stacked).astype(BF16).reshape(2, 2, 2, 80, 256)
            r1[0, 0] = units[0, 0, 0]
            t1[...] = units[0]
            t2[...] = units[1]
        else:
            units = dot(early[...], stacked).astype(BF16).reshape(2, 2, 144, 256)
            r0[0, 0] = units[0, 0]
            t0[...] = units
        for half in range(2):
            for j in range(2):
                to = 2 * half + (0 if j == 0 else 1 - 2 * odd)
                n = half * 2 + j
                if cb == 1:
                    final_copies.append(
                        send(t2.at[half, j], r2.at[half, j], s4.at[n], v4.at[n], peer(1, to)))
                    final_copies[-1].start()
                if n > 0:
                    src, dst, base = (t1, r1, 3) if cb == 1 else (t0, r0, 6)
                    final_copies.append(
                        send(src.at[half, j], dst.at[half, j], s4.at[base + n], v4.at[base + n], peer(0, to)))
                    final_copies[-1].start()

    for copy in final_copies:
        copy.wait_recv()
    for level in range(2):
        j = 1 - level
        parts = [r[half, j] for r in (r0, r1, r2) for half in range(2)]
        parts = jnp.concatenate(parts, axis=0)
        for n in range(4):
            out[level, :, pl.ds(256 * n, 256)] = dot(place[n], parts).astype(BF16)

    for copy in feature_copies:
        copy.wait_send()
    edge.wait_send()

    @pl.when(even)
    def _():
        for copy in even_copies:
            copy.wait_send()

    @pl.when(jnp.logical_not(even))
    def _():
        for copy in odd_copies:
            copy.wait_send()

    for copy in final_copies:
        copy.wait_send()


def body(nlat, nlon, features, packed_first, scale_first, output_first, gain_first, offset_first,
         merge_weight, merge_gain, merge_offset,
         packed_second, scale_second, output_second, gain_second, offset_second):
    any_spec = pl.BlockSpec(memory_space=pl.ANY)
    vmem = pl.BlockSpec(memory_space=pltpu.VMEM)
    dma = pltpu.SemaphoreType.DMA
    row = lambda v: v.reshape(1, -1)
    *small, keep, valid, heads = [jnp.asarray(t) for t in tables()]
    cut, pick, late, early, place = small
    out = pl.pallas_call(
        functools.partial(kernel, nlat, nlon),
        out_shape=jax.ShapeDtypeStruct((2, 144, 1024), BF16),
        in_specs=[any_spec] * 22,
        out_specs=vmem,
        scratch_shapes=[
            pltpu.VMEM((4, 12, 24, 512), BF16),
            pltpu.VMEM((512, 1536), BF16),
            pltpu.VMEM((512, 512), BF16),
            pltpu.VMEM((2048, 1024), BF16),
            pltpu.VMEM((1024, 1536), BF16),
            pltpu.VMEM((512, 1024), BF16),
            pltpu.VMEM((320, 320), BF16),
            pltpu.VMEM((640, 640), BF16),
            pltpu.VMEM((576, 640), BF16),
            pltpu.VMEM((4, 144, 608), BF16),
            pltpu.SMEM((8,), F32),
            *[pltpu.VMEM((1, 512), F32)] * 2,
            *[pltpu.VMEM((1, 1024), F32)] * 2,
            pltpu.SMEM((8,), F32),
            *[pltpu.VMEM((1, 1024), F32)] * 2,
            pltpu.VMEM((2, 160, 192), BF16),
            pltpu.VMEM((4, WIN, WIN), BF16),
            pltpu.VMEM((WIN, 128), F32),
            pltpu.VMEM((256, 256), BF16),
            pltpu.VMEM((8, 80, 512), BF16),
            pltpu.VMEM((1, 80, 512), BF16),
            pltpu.VMEM((2, 8, 80, 512), BF16),
            pltpu.VMEM((4, 2, ATOM, 1536), F32),
            pltpu.VMEM((4, 2, ATOM, 512), F32),
            pltpu.VMEM((2, 9, 80, 512), BF16),
            pltpu.VMEM((2, 160, 2048), BF16),
            pltpu.VMEM((2, 2, 80, 1024), BF16),
            pltpu.VMEM((4, 80, 1024), BF16),
            pltpu.VMEM((2, 2, 144, 256), BF16),
            pltpu.VMEM((2, 2, 80, 256), BF16),
            pltpu.VMEM((2, 2, 80, 256), BF16),
            pltpu.VMEM((2, 2, 144, 256), BF16),
            pltpu.VMEM((2, 2, 80, 256), BF16),
            pltpu.VMEM((2, 2, 80, 256), BF16),
            dma((22,)),
            dma((6,)), dma((6,)),
            dma, dma,
            dma((3,)), dma((4,)),
            dma((10,)), dma((10,)),
        ],
        compiler_params=pltpu.CompilerParams(
            collective_id=0, has_side_effects=True, vmem_limit_bytes=62 * 2**20
        ),
        cost_estimate=pl.CostEstimate(flops=6_000_000_000, bytes_accessed=14_000_000, transcendentals=2_000_000),
    )(
        jnp.transpose(features, (0, 2, 1, 3)), packed_first, output_first, merge_weight, packed_second, output_second,
        pick, late, early, place,
        scale_first, row(gain_first), row(offset_first), row(merge_gain), row(merge_offset),
        scale_second, row(gain_second), row(offset_second),
        cut, keep, valid, heads,
    )
    return jnp.transpose(out.reshape(2, 12, 1, 12, 1024), (1, 2, 0, 3, 4))


def solution(mesh):
    return jax.shard_map(
        functools.partial(body, mesh.shape["lat"], mesh.shape["lon"]),
        mesh=mesh,
        in_specs=(P(None, "lat", "lon", None),) + (P(),) * 13,
        out_specs=P("lat", "lon", None, None, None),
        check_vma=False,
    )
```

```python
import functools

import jax
import jax.numpy as jnp
import numpy as np
from jax import lax
from jax.experimental import pallas as pl
from jax.experimental.pallas import tpu as pltpu
from jax.sharding import PartitionSpec as P

ATOM = 40
CELLS = 36
WIN = 4 * ATOM
MESH = pl.DeviceIdType.MESH
BF16 = jnp.bfloat16
F32 = jnp.float32
LOG2E = 1.4426950408889634
NORM_EPS = 1e-05
UNIT_EPS = 1e-06


def level_of(p, j):
    return (2 * p + j + 1) % 4


@functools.lru_cache(None)
def tables():
    cut = np.zeros((2, 160, 192), np.float32)
    for part in range(2):
        for hb in range(4):
            for i in range(3):
                for j in range(2):
                    for c in range(6):
                        row = hb * 40 + (i * 2 + j) * 6 + c
                        cut[part, row, (j * 6 + c) * 16 + 3 * hb + i + 4 * part] = 1
    pick = np.zeros((3, 160, 240), np.float32)
    for cp in range(2):
        for rp in range(2):
            for u in range(2):
                for i in range(3):
                    for j in range(2):
                        for c in range(3):
                            row = (cp * 2 + rp) * 40 + u * 18 + (i * 2 + j) * 3 + c
                            fine = 6 * u + 2 * i + rp
                            hb, at = 1 + fine // 3, (fine % 3 * 2 + j) * 6 + 2 * c + cp
                            pick[0, row, hb * 40 + at] = 1
                            for p in range(2):
                                pick[1 + p, row, (hb * 40 if hb < 4 else 160 + p * 40) + at] = 1
    late = np.zeros((320, 320), np.float32)
    early = np.zeros((288, 320), np.float32)
    for lane in range(4):
        for u in range(2):
            for j in range(2):
                for i in range(3):
                    for c in range(6):
                        src = lane * 80 + c // 3 * 40 + u * 18 + (i * 2 + j) * 3 + c % 3
                        late[(u * 2 + j) * 80 + lane * 18 + i * 6 + c, src] = 1
                        early[j * 144 + lane * 36 + u * 18 + i * 6 + c, src] = 1
    place = np.zeros((4, 144, 608), np.float32)
    for lane in range(4):
        for row in range(12):
            for col in range(12):
                half, c = (1, col) if col < 6 else (0, col - 6)
                if row < 3:
                    src = 448 + 80 * half + lane * 18 + row * 6 + c
                elif row < 9:
                    src = 144 * half + lane * 36 + (row - 3) * 6 + c
                else:
                    src = 288 + 80 * half + lane * 18 + (row - 9) * 6 + c
                place[lane, row * 12 + col, src] = 1
    t = np.arange(WIN) % ATOM
    atom = np.arange(WIN) // ATOM
    keep = np.stack(
        [
            (t // 6 % 2)[:, None] == (t // 6 % 2)[None],
            (atom % 2)[:, None] == (atom % 2)[None],
            (t % 18 // 3 % 2)[:, None] == (t % 18 // 3 % 2)[None],
            (t < 18)[:, None] == (t < 18)[None],
        ]
    ).astype(np.float32)
    valid = np.broadcast_to((t < CELLS)[:, None], (WIN, 128)).astype(np.float32)
    low = (np.arange(128) < 64)[None].astype(np.float32)
    sides = np.stack([valid * low, valid * (1 - low)])
    group = np.arange(256) // 64
    heads = (group[:, None] == group[None]).astype(np.float32)
    b = lambda x: x.astype(jnp.bfloat16)
    return b(cut), b(pick), b(late), b(early), b(place), b(keep), b(sides), b(heads)


def layer_norm(values, gain, offset):
    average = jnp.mean(values, axis=-1, keepdims=True)
    centred = values - average
    spread = jnp.mean(centred * centred, axis=-1, keepdims=True)
    return centred * lax.rsqrt(spread + NORM_EPS) * gain + offset


def dot(a, b):
    return jnp.dot(a, b, preferred_element_type=F32)


def project(x, weight_ref, heads_ref, store):
    for at in range(3):
        y = dot(x, weight_ref[:, pl.ds(512 * at, 512)]).astype(BF16)
        if at < 2:
            squares = y * y
            total = jnp.concatenate(
                [dot(squares[:, :256], heads_ref[...]), dot(squares[:, 256:], heads_ref[...])], axis=1
            )
            y = (y.astype(F32) * lax.rsqrt(total + UNIT_EPS)).astype(BF16)
        store(512 * at, y)


def attend(fetch, store, mask, sides_ref, scale_ref):
    low = lax.broadcasted_iota(jnp.int32, (WIN, 128), 1) < 64
    for g in range(4):
        q, k, v = fetch(128 * g), fetch(512 + 128 * g), fetch(1024 + 128 * g)
        parts = []
        for side in range(2):
            key = k * sides_ref[side]
            value = v * sides_ref[side] + sides_ref[1 - side]
            score = lax.dot_general(q, key, (((1,), (1,)), ((), ())), preferred_element_type=F32)
            weight = jnp.exp2(score * (scale_ref[2 * g + side] * LOG2E)).astype(BF16)
            parts.append(dot(weight if mask is None else weight * mask, value))
        top = jnp.where(low, parts[0], parts[1])
        total = pltpu.roll(jnp.where(low, parts[1], parts[0]), 64, 1)
        store(128 * g, (top / total).astype(BF16))


def kernel(
    nlat, nlon,
    feat_hbm, packed1_hbm, out1_hbm, merge_hbm, packed2_hbm, out2_hbm,
    pick_hbm, late_hbm, early_hbm, place_hbm,
    scale1_hbm, gain1_hbm, offset1_hbm, gainm_hbm, offsetm_hbm, scale2_hbm, gain2_hbm, offset2_hbm,
    cut_hbm, keep_hbm, sides_hbm, heads_hbm,
    out,
    feat, packed1, wout1, wmerge, packed2, wout2, pick, late, early, place,
    scale1, gain1, offset1, gainm, offsetm, scale2, gain2, offset2, cut, keep, sides, heads,
    send0, send7, send_row, send_corner, x, rim, yn, ctx, first, edge_out, edge_in, picked, mb, quarter, t0, t1, t2, r0, r1, r2,
    load_sem, s1, v1, s2, v2, s3, v3, s4, v4,
):
    lat, lon = lax.axis_index("lat"), lax.axis_index("lon")
    odd = lax.rem(lon, 2)
    even = odd == 0

    def peer(dlat, dlon):
        return (lax.rem(lat + dlat + nlat, nlat), lax.rem(lon + dlon + nlon, nlon))

    def send(src, dst, send_sem, recv_sem, where):
        return pltpu.make_async_remote_copy(
            src_ref=src, dst_ref=dst, send_sem=send_sem, recv_sem=recv_sem,
            device_id=where, device_id_type=MESH,
        )

    def load(*pairs):
        copies = [pltpu.make_async_copy(a, b, load_sem.at[order.pop()]) for a, b in pairs]
        for copy in copies:
            copy.start()

        def wait():
            for copy in copies:
                copy.wait()

        return wait

    order = list(range(22))
    cut_loaded = load((feat_hbm, feat), (cut_hbm, cut))
    barrier = pltpu.get_barrier_semaphore()
    for dlat, dlon in [
        (0, 1), (0, -1), (0, -2), (1, 0), (1, 1), (-1, 0), (-1, -1), (-1, -2),
        (0, jnp.where(even, 2, -3)), (-1, jnp.where(even, 1, -3)),
    ]:
        pl.semaphore_signal(barrier, inc=1, device_id=peer(dlat, dlon), device_id_type=MESH)

    first_loaded = load(
        (packed1_hbm, packed1), (heads_hbm, heads), (keep_hbm, keep), (sides_hbm, sides), (scale1_hbm, scale1),
        (out1_hbm, wout1), (gain1_hbm, gain1), (offset1_hbm, offset1),
    )
    merge_loaded = load((pick_hbm, pick), (merge_hbm, wmerge), (gainm_hbm, gainm), (offsetm_hbm, offsetm))
    second_loaded = load(
        (packed2_hbm, packed2), (out2_hbm, wout2), (scale2_hbm, scale2), (gain2_hbm, gain2), (offset2_hbm, offset2),
        (late_hbm, late), (early_hbm, early), (place_hbm, place),
    )

    cut_loaded()

    feature_copies = [
        send(send0.at[n], x.at[n, 1], s1.at[n], v1.at[n], peer(0, -1)) for n in range(3)
    ] + [
        send(send7, rim.at[1, 0], s1.at[3], v1.at[3], peer(0, -1)),
        send(send_corner, rim.at[1, 1], s1.at[4], v1.at[4], peer(-1, -1)),
        send(send_row, rim.at[0, 1], s1.at[5], v1.at[5], peer(-1, 0)),
    ]

    def atoms_of(half, p, part):
        tokens = jnp.stack([
            feat[level_of(p, j), 6 * half : 6 * half + 6].astype(F32)[:, 8 * part : 8 * part + 16]
            for j in range(2)
        ]).astype(BF16).reshape(192, 512)
        return dot(cut[part], tokens).reshape(4, ATOM, 512)

    for half in range(2):
        upper = [atoms_of(half, p, 0) for p in range(2)]
        if half == 0:
            for p in range(2):
                send0[0, p] = upper[p][1:3].reshape(80, 512).astype(BF16)
            pl.semaphore_wait(barrier, jnp.where(even, 11, 9))
            feature_copies[0].start()
        lower = [atoms_of(half, p, 1) for p in range(2)]
        ends = [jnp.concatenate([a[n] for a in side], axis=0).astype(BF16) for side, n in ((upper, 0), (lower, 3))]
        for p in range(2):
            second = jnp.concatenate([upper[p][3], lower[p][0]], axis=0).astype(BF16)
            third = lower[p][1:3].reshape(80, 512).astype(BF16)
            if half == 0:
                send0[1, p] = second
                send0[2, p] = third
            else:
                x[0, 0, p] = upper[p][1:3].reshape(80, 512).astype(BF16)
                x[1, 0, p] = second
                x[2, 0, p] = third
        if half == 0:
            send7[...] = ends[1]
            send_corner[...] = ends[0]
            for copy in feature_copies[1:5]:
                copy.start()
        else:
            send_row[...] = ends[0]
            feature_copies[5].start()
            rim[0, 0] = ends[1]

    first_loaded()
    edge = send(edge_out, edge_in, s2, v2, peer(-1, 0))
    last_lat = lat == nlat - 1

    even_copies = [
        [
            send(mb.at[cb, 0, 0], quarter.at[cb, 3], s3.at[cb, 0], v3.at[cb, 3], peer(0, -2)),
            send(mb.at[cb, 0, 1], quarter.at[cb, 3], s3.at[cb, 1], v3.at[cb, 3], peer(0, -1)),
            send(mb.at[cb, 1, 1], quarter.at[cb, 0], s3.at[cb, 2], v3.at[cb, 0], peer(0, 1)),
        ]
        for cb in range(2)
    ]
    odd_copies = [
        [
            send(mb.at[cb, 0, 0], quarter.at[cb, 1], s3.at[cb, 0], v3.at[cb, 1], peer(0, -1)),
            send(mb.at[cb, 1, 0], quarter.at[cb, 2], s3.at[cb, 1], v3.at[cb, 2], peer(0, -1)),
        ]
        for cb in range(2)
    ]

    def merge(cb):
        for half in range(2):
            parts = []
            for p in range(2):
                if cb == 0:
                    moved = dot(pick[0], first[0:3, half, p].reshape(240, 512))
                else:
                    fine = jnp.concatenate([first[2:4, half, p].reshape(160, 512), edge_in[half]], axis=0)
                    moved = dot(pick[1 + p], fine)
                parts.append(moved.reshape(4, ATOM, 512))
            parts = jnp.concatenate(parts, axis=1).astype(BF16)
            for at in range(4):
                picked[cb, pl.ds(80 * half, 80), pl.ds(512 * at, 512)] = parts[at]
        normed = layer_norm(dot(picked[cb], wmerge[...]), gainm[...], offsetm[...])
        for half in range(2):
            for p in range(2):
                rows = normed[(half * 2 + p) * ATOM : (half * 2 + p + 1) * ATOM]
                mb[cb, half, p] = jnp.concatenate([rows[:, :512], rows[:, 512:]], axis=0).astype(BF16)

        @pl.when(even)
        def _():
            for copy in even_copies[cb]:
                copy.start()
            quarter[cb, 0] = mb[cb, 1, 0]

        @pl.when(jnp.logical_not(even))
        def _():
            for copy in odd_copies[cb]:
                copy.start()
            quarter[cb, 1] = mb[cb, 0, 1]
            quarter[cb, 2] = mb[cb, 1, 1]

    def merged_arrived(cb):
        @pl.when(even)
        def _():
            odd_copies[cb][0].wait_recv()
            odd_copies[cb][1].wait_recv()

        @pl.when(jnp.logical_not(even))
        def _():
            even_copies[cb][2].wait_recv()

        even_copies[cb][0].wait_recv()

    def band(b, carry):
        for n in range(3):
            @pl.when(b == n)
            def _():
                feature_copies[n].wait_recv()

        @pl.when(b == 3)
        def _():
            for n in range(3, 6):
                feature_copies[n].wait_recv()
            for half in range(2):
                near, far = rim[half, 0].astype(F32), rim[half, 1].astype(F32)
                for p in range(2):
                    rows = slice(ATOM * p, ATOM * p + ATOM)
                    x[3, half, p] = jnp.concatenate([near[rows], far[rows]], axis=0).astype(BF16)

        xb = x[b].reshape(320, 512)

        def keep_rows(at, y):
            yn[:, :, :, pl.ds(at, 512)] = y.reshape(2, 2, 80, 512)

        project(xb, packed1, heads, keep_rows)
        wrapped = jnp.where(jnp.logical_and(last_lat, b == 3), 1.0, 0.0).astype(F32)
        rows = keep[1].astype(F32) * wrapped + (1.0 - wrapped)
        for p in range(2):
            def fetch(at):
                return yn[:, p, :, pl.ds(at, 128)].reshape(WIN, 128)

            def keep_context(at, value):
                ctx[:, p, :, pl.ds(at, 128)] = value.reshape(2, 80, 128)

            mask = rows if p == 0 else rows * keep[0].astype(F32)
            attend(fetch, keep_context, mask.astype(BF16), sides, scale1)
        branch = layer_norm(dot(ctx[...].reshape(320, 512), wout1[...]), gain1[...], offset1[...])
        result = (xb.astype(F32) + branch).reshape(2, 2, 80, 512)
        first[b] = result.astype(BF16)

        @pl.when(b == 0)
        def _():
            edge_out[...] = result[:, :, :ATOM].reshape(2, 80, 512).astype(BF16)
            edge.start()

        @pl.when(b == 2)
        def _():
            merge_loaded()
            merge(0)
        return carry

    lax.fori_loop(0, 4, band, 0)

    edge.wait_recv()
    merge(1)

    second_loaded()
    odd_half = odd.astype(F32)
    levels = keep[2].astype(F32) * odd_half + (1.0 - odd_half)

    def keep_rows(at, y):
        yn[0, :, :, pl.ds(at, 512)] = y.reshape(2, 80, 512)

    def fetch(at):
        return yn[0, :, :, pl.ds(at, 128)].reshape(WIN, 128)

    def keep_context(at, value):
        ctx[0, :, :, pl.ds(at, 128)] = value.reshape(2, 80, 128)

    final_copies = []
    for cb in range(2):
        merged_arrived(cb)
        if cb == 1:
            wrapped = jnp.where(last_lat, 1.0, 0.0).astype(F32)
            mask = levels * (keep[3].astype(F32) * wrapped + (1.0 - wrapped))
        else:
            mask = levels
        own = [quarter[cb, n].astype(F32) for n in range(4)]
        own = jnp.concatenate([jnp.concatenate([q[:ATOM], q[ATOM:]], axis=1) for q in own], axis=0)
        project(own.astype(BF16), packed2, heads, keep_rows)
        attend(fetch, keep_context, mask.astype(BF16), sides, scale2)
        for half in (1, 0):
            branch = layer_norm(dot(ctx[0, half], wout2[...]), gain2[...], offset2[...])
            second = (own[80 * half : 80 * half + 80] + branch).astype(BF16)
            stacked = jnp.concatenate([second[:, 256 * n : 256 * n + 256] for n in range(4)], axis=0)
            if cb == 1:
                units = dot(late[...], stacked).astype(BF16).reshape(2, 2, 80, 256)
                if half == 0:
                    r1[0, 0] = units[0, 0]
                t1[half] = units[0]
                t2[half] = units[1]
            else:
                units = dot(early[...], stacked).astype(BF16).reshape(2, 144, 256)
                if half == 0:
                    r0[0, 0] = units[0]
                t0[half] = units
            for j in range(2):
                to = 2 * half + (0 if j == 0 else 1 - 2 * odd)
                n = half * 2 + j
                if cb == 1:
                    final_copies.append(
                        send(t2.at[half, j], r2.at[half, j], s4.at[n], v4.at[n], peer(1, to)))
                    final_copies[-1].start()
                if n > 0:
                    src, dst, base = (t1, r1, 3) if cb == 1 else (t0, r0, 6)
                    final_copies.append(
                        send(src.at[half, j], dst.at[half, j], s4.at[base + n], v4.at[base + n], peer(0, to)))
                    final_copies[-1].start()

    for copy in final_copies:
        copy.wait_recv()
    for level in range(2):
        j = 1 - level
        parts = [r[half, j] for r in (r0, r1, r2) for half in range(2)]
        parts = jnp.concatenate(parts, axis=0)
        for n in range(4):
            out[level, :, pl.ds(256 * n, 256)] = dot(place[n], parts).astype(BF16)

    for copy in feature_copies:
        copy.wait_send()
    edge.wait_send()

    @pl.when(even)
    def _():
        for copy in even_copies[0] + even_copies[1]:
            copy.wait_send()

    @pl.when(jnp.logical_not(even))
    def _():
        for copy in odd_copies[0] + odd_copies[1]:
            copy.wait_send()

    for copy in final_copies:
        copy.wait_send()


def body(nlat, nlon, features, packed_first, scale_first, output_first, gain_first, offset_first,
         merge_weight, merge_gain, merge_offset,
         packed_second, scale_second, output_second, gain_second, offset_second):
    any_spec = pl.BlockSpec(memory_space=pl.ANY)
    vmem = pl.BlockSpec(memory_space=pltpu.VMEM)
    dma = pltpu.SemaphoreType.DMA
    row = lambda v: v.reshape(1, -1)
    *small, keep, sides, heads = [jnp.asarray(t) for t in tables()]
    cut, pick, late, early, place = small
    out = pl.pallas_call(
        functools.partial(kernel, nlat, nlon),
        out_shape=jax.ShapeDtypeStruct((2, 144, 1024), BF16),
        in_specs=[any_spec] * 22,
        out_specs=vmem,
        scratch_shapes=[
            pltpu.VMEM((4, 12, 24, 512), BF16),
            pltpu.VMEM((512, 1536), BF16),
            pltpu.VMEM((512, 512), BF16),
            pltpu.VMEM((2048, 1024), BF16),
            pltpu.VMEM((1024, 1536), BF16),
            pltpu.VMEM((512, 1024), BF16),
            pltpu.VMEM((3, 160, 240), BF16),
            pltpu.VMEM((320, 320), BF16),
            pltpu.VMEM((288, 320), BF16),
            pltpu.VMEM((4, 144, 608), BF16),
            pltpu.SMEM((8,), F32),
            *[pltpu.VMEM((1, 512), F32)] * 2,
            *[pltpu.VMEM((1, 1024), F32)] * 2,
            pltpu.SMEM((8,), F32),
            *[pltpu.VMEM((1, 1024), F32)] * 2,
            pltpu.VMEM((2, 160, 192), BF16),
            pltpu.VMEM((4, WIN, WIN), BF16),
            pltpu.VMEM((2, WIN, 128), BF16),
            pltpu.VMEM((256, 256), BF16),
            pltpu.VMEM((3, 2, 80, 512), BF16),
            pltpu.VMEM((80, 512), BF16),
            pltpu.VMEM((80, 512), BF16),
            pltpu.VMEM((80, 512), BF16),
            pltpu.VMEM((4, 2, 2, 80, 512), BF16),
            pltpu.VMEM((2, 2, 80, 512), BF16),
            pltpu.VMEM((2, 2, 80, 1536), BF16),
            pltpu.VMEM((2, 2, 80, 512), BF16),
            pltpu.VMEM((4, 2, 2, 80, 512), BF16),
            pltpu.VMEM((2, 80, 512), BF16),
            pltpu.VMEM((2, 80, 512), BF16),
            pltpu.VMEM((2, 160, 2048), BF16),
            pltpu.VMEM((2, 2, 2, 80, 512), BF16),
            pltpu.VMEM((2, 4, 80, 512), BF16),
            pltpu.VMEM((2, 2, 144, 256), BF16),
            pltpu.VMEM((2, 2, 80, 256), BF16),
            pltpu.VMEM((2, 2, 80, 256), BF16),
            pltpu.VMEM((2, 2, 144, 256), BF16),
            pltpu.VMEM((2, 2, 80, 256), BF16),
            pltpu.VMEM((2, 2, 80, 256), BF16),
            dma((22,)),
            dma((6,)), dma((6,)),
            dma, dma,
            dma((2, 3)), dma((2, 4)),
            dma((10,)), dma((10,)),
        ],
        compiler_params=pltpu.CompilerParams(
            collective_id=0, has_side_effects=True, vmem_limit_bytes=62 * 2**20
        ),
        cost_estimate=pl.CostEstimate(flops=6_000_000_000, bytes_accessed=14_000_000, transcendentals=2_000_000),
    )(
        jnp.transpose(features, (0, 2, 1, 3)), packed_first, output_first, merge_weight, packed_second, output_second,
        pick, late, early, place,
        scale_first, row(gain_first), row(offset_first), row(merge_gain), row(merge_offset),
        scale_second, row(gain_second), row(offset_second),
        cut, keep, sides, heads,
    )
    return jnp.transpose(out.reshape(2, 12, 1, 12, 1024), (1, 2, 0, 3, 4))


def solution(mesh):
    return jax.shard_map(
        functools.partial(body, mesh.shape["lat"], mesh.shape["lon"]),
        mesh=mesh,
        in_specs=(P(None, "lat", "lon", None),) + (P(),) * 13,
        out_specs=P("lat", "lon", None, None, None),
        check_vma=False,
    )
```

```python
import functools

import jax
import jax.numpy as jnp
import numpy as np
from jax import lax
from jax.experimental import pallas as pl
from jax.experimental.pallas import tpu as pltpu
from jax.sharding import PartitionSpec as P

ATOM = 40
CELLS = 36
WIN = 4 * ATOM
MESH = pl.DeviceIdType.MESH
BF16 = jnp.bfloat16
F32 = jnp.float32
LOG2E = 1.4426950408889634
NORM_EPS = 1e-05
UNIT_EPS = 1e-06


def level_of(p, j):
    return (2 * p + j + 1) % 4


@functools.lru_cache(None)
def tables():
    cut = np.zeros((2, 160, 192), np.float32)
    for part in range(2):
        for hb in range(4):
            for i in range(3):
                for j in range(2):
                    for c in range(6):
                        row = hb * 40 + (i * 2 + j) * 6 + c
                        cut[part, row, (j * 6 + c) * 16 + 3 * hb + i + 4 * part] = 1
    pick = np.zeros((3, 160, 240), np.float32)
    for cp in range(2):
        for rp in range(2):
            for u in range(2):
                for i in range(3):
                    for j in range(2):
                        for c in range(3):
                            row = (cp * 2 + rp) * 40 + u * 18 + (i * 2 + j) * 3 + c
                            fine = 6 * u + 2 * i + rp
                            hb, at = 1 + fine // 3, (fine % 3 * 2 + j) * 6 + 2 * c + cp
                            pick[0, row, hb * 40 + at] = 1
                            for p in range(2):
                                pick[1 + p, row, (hb * 40 if hb < 4 else 160 + p * 40) + at] = 1
    late = np.zeros((320, 320), np.float32)
    early = np.zeros((288, 320), np.float32)
    for lane in range(4):
        for u in range(2):
            for j in range(2):
                for i in range(3):
                    for c in range(6):
                        src = lane * 80 + c // 3 * 40 + u * 18 + (i * 2 + j) * 3 + c % 3
                        late[(u * 2 + j) * 80 + lane * 18 + i * 6 + c, src] = 1
                        early[j * 144 + lane * 36 + u * 18 + i * 6 + c, src] = 1
    place = np.zeros((4, 144, 608), np.float32)
    for lane in range(4):
        for row in range(12):
            for col in range(12):
                half, c = (1, col) if col < 6 else (0, col - 6)
                if row < 3:
                    src = 448 + 80 * half + lane * 18 + row * 6 + c
                elif row < 9:
                    src = 144 * half + lane * 36 + (row - 3) * 6 + c
                else:
                    src = 288 + 80 * half + lane * 18 + (row - 9) * 6 + c
                place[lane, row * 12 + col, src] = 1
    t = np.arange(WIN) % ATOM
    atom = np.arange(WIN) // ATOM
    keep = np.stack(
        [
            (t // 6 % 2)[:, None] == (t // 6 % 2)[None],
            (atom % 2)[:, None] == (atom % 2)[None],
            (t % 18 // 3 % 2)[:, None] == (t % 18 // 3 % 2)[None],
            (t < 18)[:, None] == (t < 18)[None],
        ]
    ).astype(np.float32)
    valid = np.broadcast_to((t < CELLS)[:, None], (WIN, 128)).astype(np.float32)
    low = (np.arange(128) < 64)[None].astype(np.float32)
    sides = np.stack([valid * low, valid * (1 - low)])
    group = np.arange(256) // 64
    heads = (group[:, None] == group[None]).astype(np.float32)
    b = lambda x: x.astype(jnp.bfloat16)
    return b(cut), b(pick), b(late), b(early), b(place), b(keep), b(sides), b(heads)


def layer_norm(values, gain, offset):
    average = jnp.mean(values, axis=-1, keepdims=True)
    centred = values - average
    spread = jnp.mean(centred * centred, axis=-1, keepdims=True)
    return centred * lax.rsqrt(spread + NORM_EPS) * gain + offset


def dot(a, b):
    return jnp.dot(a, b, preferred_element_type=F32)


def project(x, weight_ref, heads_ref, store):
    for at in range(3):
        y = dot(x, weight_ref[:, pl.ds(512 * at, 512)]).astype(BF16)
        if at < 2:
            squares = y * y
            total = jnp.concatenate(
                [dot(squares[:, :256], heads_ref[...]), dot(squares[:, 256:], heads_ref[...])], axis=1
            )
            y = (y.astype(F32) * lax.rsqrt(total + UNIT_EPS)).astype(BF16)
        store(512 * at, y)


def attend(fetch, store, mask, sides_ref, scale_ref):
    low = lax.broadcasted_iota(jnp.int32, (WIN, 128), 1) < 64
    for g in range(4):
        q, k, v = fetch(128 * g), fetch(512 + 128 * g), fetch(1024 + 128 * g)
        parts = []
        for side in range(2):
            key = k * sides_ref[side]
            value = v * sides_ref[side] + sides_ref[1 - side]
            score = lax.dot_general(q, key, (((1,), (1,)), ((), ())), preferred_element_type=F32)
            weight = jnp.exp2(score * (scale_ref[2 * g + side] * LOG2E)).astype(BF16)
            parts.append(dot(weight if mask is None else weight * mask, value))
        top = jnp.where(low, parts[0], parts[1])
        total = pltpu.roll(jnp.where(low, parts[1], parts[0]), 64, 1)
        store(128 * g, (top / total).astype(BF16))


def kernel(
    nlat, nlon,
    feat_hbm, packed1_hbm, out1_hbm, merge_hbm, packed2_hbm, out2_hbm,
    pick_hbm, late_hbm, early_hbm, place_hbm,
    scale1_hbm, gain1_hbm, offset1_hbm, gainm_hbm, offsetm_hbm, scale2_hbm, gain2_hbm, offset2_hbm,
    cut_hbm, keep_hbm, sides_hbm, heads_hbm,
    out,
    feat, packed1, wout1, wmerge, packed2, wout2, pick, late, early, place,
    scale1, gain1, offset1, gainm, offsetm, scale2, gain2, offset2, cut, keep, sides, heads,
    send0, send7, send_row, send_corner, x, rim, yn, ctx, first, edge_out, edge_in, picked, mb, quarter, t0, t1, t2, r0, r1, r2,
    load_sem, s1, v1, s2, v2, s3, v3, s4, v4,
):
    lat, lon = lax.axis_index("lat"), lax.axis_index("lon")
    odd = lax.rem(lon, 2)
    even = odd == 0

    def peer(dlat, dlon):
        return (lax.rem(lat + dlat + nlat, nlat), lax.rem(lon + dlon + nlon, nlon))

    def send(src, dst, send_sem, recv_sem, where):
        return pltpu.make_async_remote_copy(
            src_ref=src, dst_ref=dst, send_sem=send_sem, recv_sem=recv_sem,
            device_id=where, device_id_type=MESH,
        )

    def load(*pairs):
        copies = [pltpu.make_async_copy(a, b, load_sem.at[order.pop()]) for a, b in pairs]
        for copy in copies:
            copy.start()

        def wait():
            for copy in copies:
                copy.wait()

        return wait

    order = list(range(22))
    cut_loaded = load((feat_hbm, feat), (cut_hbm, cut))
    barrier = pltpu.get_barrier_semaphore()
    for dlat, dlon in [
        (0, 1), (0, -1), (0, -2), (1, 0), (1, 1), (-1, 0), (-1, -1), (-1, -2),
        (0, jnp.where(even, 2, -3)), (-1, jnp.where(even, 1, -3)),
    ]:
        pl.semaphore_signal(barrier, inc=1, device_id=peer(dlat, dlon), device_id_type=MESH)

    first_loaded = load(
        (packed1_hbm, packed1), (heads_hbm, heads), (keep_hbm, keep), (sides_hbm, sides), (scale1_hbm, scale1),
        (out1_hbm, wout1), (gain1_hbm, gain1), (offset1_hbm, offset1),
    )
    merge_loaded = load((pick_hbm, pick), (merge_hbm, wmerge), (gainm_hbm, gainm), (offsetm_hbm, offsetm))
    second_loaded = load(
        (packed2_hbm, packed2), (out2_hbm, wout2), (scale2_hbm, scale2), (gain2_hbm, gain2), (offset2_hbm, offset2),
        (late_hbm, late), (early_hbm, early), (place_hbm, place),
    )

    cut_loaded()

    feature_copies = [
        send(send0.at[n], x.at[n, 1], s1.at[n], v1.at[n], peer(0, -1)) for n in range(3)
    ] + [
        send(send7, rim.at[1, 0], s1.at[3], v1.at[3], peer(0, -1)),
        send(send_corner, rim.at[1, 1], s1.at[4], v1.at[4], peer(-1, -1)),
        send(send_row, rim.at[0, 1], s1.at[5], v1.at[5], peer(-1, 0)),
    ]

    def atoms_of(half, p, part):
        tokens = jnp.stack([
            feat[level_of(p, j), 6 * half : 6 * half + 6].astype(F32)[:, 8 * part : 8 * part + 16]
            for j in range(2)
        ]).astype(BF16).reshape(192, 512)
        return dot(cut[part], tokens).reshape(4, ATOM, 512)

    for half in range(2):
        upper = [atoms_of(half, p, 0) for p in range(2)]
        if half == 0:
            for p in range(2):
                send0[0, p] = upper[p][1:3].reshape(80, 512).astype(BF16)
            pl.semaphore_wait(barrier, jnp.where(even, 11, 9))
            feature_copies[0].start()
        lower = [atoms_of(half, p, 1) for p in range(2)]
        ends = [jnp.concatenate([a[n] for a in side], axis=0).astype(BF16) for side, n in ((upper, 0), (lower, 3))]
        for p in range(2):
            second = jnp.concatenate([upper[p][3], lower[p][0]], axis=0).astype(BF16)
            third = lower[p][1:3].reshape(80, 512).astype(BF16)
            if half == 0:
                send0[1, p] = second
                send0[2, p] = third
            else:
                x[0, 0, p] = upper[p][1:3].reshape(80, 512).astype(BF16)
                x[1, 0, p] = second
                x[2, 0, p] = third
        if half == 0:
            send7[...] = ends[1]
            send_corner[...] = ends[0]
            for copy in feature_copies[1:5]:
                copy.start()
        else:
            send_row[...] = ends[0]
            feature_copies[5].start()
            rim[0, 0] = ends[1]

    first_loaded()
    edge = send(edge_out, edge_in, s2, v2, peer(-1, 0))
    last_lat = lat == nlat - 1

    even_copies = [
        [
            send(mb.at[cb, 0, 0], quarter.at[cb, 3], s3.at[cb, 0], v3.at[cb, 3], peer(0, -2)),
            send(mb.at[cb, 0, 1], quarter.at[cb, 3], s3.at[cb, 1], v3.at[cb, 3], peer(0, -1)),
            send(mb.at[cb, 1, 1], quarter.at[cb, 0], s3.at[cb, 2], v3.at[cb, 0], peer(0, 1)),
        ]
        for cb in range(2)
    ]
    odd_copies = [
        [
            send(mb.at[cb, 0, 0], quarter.at[cb, 1], s3.at[cb, 0], v3.at[cb, 1], peer(0, -1)),
            send(mb.at[cb, 1, 0], quarter.at[cb, 2], s3.at[cb, 1], v3.at[cb, 2], peer(0, -1)),
        ]
        for cb in range(2)
    ]

    def merge(cb):
        for half in range(2):
            parts = []
            for p in range(2):
                if cb == 0:
                    moved = dot(pick[0], first[0:3, half, p].reshape(240, 512))
                else:
                    fine = jnp.concatenate([first[2:4, half, p].reshape(160, 512), edge_in[half]], axis=0)
                    moved = dot(pick[1 + p], fine)
                parts.append(moved.reshape(4, ATOM, 512))
            parts = jnp.concatenate(parts, axis=1).astype(BF16)
            for at in range(4):
                picked[cb, pl.ds(80 * half, 80), pl.ds(512 * at, 512)] = parts[at]
        normed = layer_norm(dot(picked[cb], wmerge[...]), gainm[...], offsetm[...])
        for half in range(2):
            for p in range(2):
                rows = normed[(half * 2 + p) * ATOM : (half * 2 + p + 1) * ATOM]
                mb[cb, half, p] = jnp.concatenate([rows[:, :512], rows[:, 512:]], axis=0).astype(BF16)

        @pl.when(even)
        def _():
            for copy in even_copies[cb]:
                copy.start()
            quarter[cb, 0] = mb[cb, 1, 0]

        @pl.when(jnp.logical_not(even))
        def _():
            for copy in odd_copies[cb]:
                copy.start()
            quarter[cb, 1] = mb[cb, 0, 1]
            quarter[cb, 2] = mb[cb, 1, 1]

    def merged_arrived(cb):
        @pl.when(even)
        def _():
            odd_copies[cb][0].wait_recv()
            odd_copies[cb][1].wait_recv()

        @pl.when(jnp.logical_not(even))
        def _():
            even_copies[cb][2].wait_recv()

        even_copies[cb][0].wait_recv()

    def band(b, carry):
        for n in range(3):
            @pl.when(b == n)
            def _():
                feature_copies[n].wait_recv()

        @pl.when(b == 3)
        def _():
            for n in range(3, 6):
                feature_copies[n].wait_recv()
            for half in range(2):
                near, far = rim[half, 0].astype(F32), rim[half, 1].astype(F32)
                for p in range(2):
                    rows = slice(ATOM * p, ATOM * p + ATOM)
                    x[3, half, p] = jnp.concatenate([near[rows], far[rows]], axis=0).astype(BF16)

        xb = x[b].reshape(320, 512)

        def keep_rows(at, y):
            yn[:, :, :, pl.ds(at, 512)] = y.reshape(2, 2, 80, 512)

        project(xb, packed1, heads, keep_rows)
        wrapped = jnp.where(jnp.logical_and(last_lat, b == 3), 1.0, 0.0).astype(F32)
        rows = keep[1].astype(F32) * wrapped + (1.0 - wrapped)
        for p in range(2):
            def fetch(at):
                return yn[:, p, :, pl.ds(at, 128)].reshape(WIN, 128)

            def keep_context(at, value):
                ctx[:, p, :, pl.ds(at, 128)] = value.reshape(2, 80, 128)

            mask = rows if p == 0 else rows * keep[0].astype(F32)
            attend(fetch, keep_context, mask.astype(BF16), sides, scale1)
        branch = layer_norm(dot(ctx[...].reshape(320, 512), wout1[...]), gain1[...], offset1[...])
        result = (xb.astype(F32) + branch).reshape(2, 2, 80, 512)
        first[b] = result.astype(BF16)

        @pl.when(b == 0)
        def _():
            edge_out[...] = result[:, :, :ATOM].reshape(2, 80, 512).astype(BF16)

        @pl.when(b == 1)
        def _():
            edge.start()

        @pl.when(b == 2)
        def _():
            merge_loaded()
            merge(0)
        return carry

    lax.fori_loop(0, 4, band, 0)

    edge.wait_recv()
    merge(1)

    second_loaded()
    odd_half = odd.astype(F32)
    levels = keep[2].astype(F32) * odd_half + (1.0 - odd_half)

    def keep_rows(at, y):
        yn[0, :, :, pl.ds(at, 512)] = y.reshape(2, 80, 512)

    def fetch(at):
        return yn[0, :, :, pl.ds(at, 128)].reshape(WIN, 128)

    def keep_context(at, value):
        ctx[0, :, :, pl.ds(at, 128)] = value.reshape(2, 80, 128)

    final_copies = []
    for cb in range(2):
        merged_arrived(cb)
        if cb == 1:
            wrapped = jnp.where(last_lat, 1.0, 0.0).astype(F32)
            mask = levels * (keep[3].astype(F32) * wrapped + (1.0 - wrapped))
        else:
            mask = levels
        own = [quarter[cb, n].astype(F32) for n in range(4)]
        own = jnp.concatenate([jnp.concatenate([q[:ATOM], q[ATOM:]], axis=1) for q in own], axis=0)
        project(own.astype(BF16), packed2, heads, keep_rows)
        attend(fetch, keep_context, mask.astype(BF16), sides, scale2)
        for half in (1, 0):
            branch = layer_norm(dot(ctx[0, half], wout2[...]), gain2[...], offset2[...])
            second = (own[80 * half : 80 * half + 80] + branch).astype(BF16)
            stacked = jnp.concatenate([second[:, 256 * n : 256 * n + 256] for n in range(4)], axis=0)
            if cb == 1:
                units = dot(late[...], stacked).astype(BF16).reshape(2, 2, 80, 256)
                if half == 0:
                    r1[0, 0] = units[0, 0]
                t1[half] = units[0]
                t2[half] = units[1]
            else:
                units = dot(early[...], stacked).astype(BF16).reshape(2, 144, 256)
                if half == 0:
                    r0[0, 0] = units[0]
                t0[half] = units
            for j in range(2):
                to = 2 * half + (0 if j == 0 else 1 - 2 * odd)
                n = half * 2 + j
                if cb == 1:
                    final_copies.append(
                        send(t2.at[half, j], r2.at[half, j], s4.at[n], v4.at[n], peer(1, to)))
                    final_copies[-1].start()
                if n > 0:
                    src, dst, base = (t1, r1, 3) if cb == 1 else (t0, r0, 6)
                    final_copies.append(
                        send(src.at[half, j], dst.at[half, j], s4.at[base + n], v4.at[base + n], peer(0, to)))
                    final_copies[-1].start()

    for copy in final_copies:
        copy.wait_recv()
    for level in range(2):
        j = 1 - level
        parts = [r[half, j] for r in (r0, r1, r2) for half in range(2)]
        parts = jnp.concatenate(parts, axis=0)
        for n in range(4):
            out[level, :, pl.ds(256 * n, 256)] = dot(place[n], parts).astype(BF16)

    for copy in feature_copies:
        copy.wait_send()
    edge.wait_send()

    @pl.when(even)
    def _():
        for copy in even_copies[0] + even_copies[1]:
            copy.wait_send()

    @pl.when(jnp.logical_not(even))
    def _():
        for copy in odd_copies[0] + odd_copies[1]:
            copy.wait_send()

    for copy in final_copies:
        copy.wait_send()


def body(nlat, nlon, features, packed_first, scale_first, output_first, gain_first, offset_first,
         merge_weight, merge_gain, merge_offset,
         packed_second, scale_second, output_second, gain_second, offset_second):
    any_spec = pl.BlockSpec(memory_space=pl.ANY)
    vmem = pl.BlockSpec(memory_space=pltpu.VMEM)
    dma = pltpu.SemaphoreType.DMA
    row = lambda v: v.reshape(1, -1)
    *small, keep, sides, heads = [jnp.asarray(t) for t in tables()]
    cut, pick, late, early, place = small
    out = pl.pallas_call(
        functools.partial(kernel, nlat, nlon),
        out_shape=jax.ShapeDtypeStruct((2, 144, 1024), BF16),
        in_specs=[any_spec] * 22,
        out_specs=vmem,
        scratch_shapes=[
            pltpu.VMEM((4, 12, 24, 512), BF16),
            pltpu.VMEM((512, 1536), BF16),
            pltpu.VMEM((512, 512), BF16),
            pltpu.VMEM((2048, 1024), BF16),
            pltpu.VMEM((1024, 1536), BF16),
            pltpu.VMEM((512, 1024), BF16),
            pltpu.VMEM((3, 160, 240), BF16),
            pltpu.VMEM((320, 320), BF16),
            pltpu.VMEM((288, 320), BF16),
            pltpu.VMEM((4, 144, 608), BF16),
            pltpu.SMEM((8,), F32),
            *[pltpu.VMEM((1, 512), F32)] * 2,
            *[pltpu.VMEM((1, 1024), F32)] * 2,
            pltpu.SMEM((8,), F32),
            *[pltpu.VMEM((1, 1024), F32)] * 2,
            pltpu.VMEM((2, 160, 192), BF16),
            pltpu.VMEM((4, WIN, WIN), BF16),
            pltpu.VMEM((2, WIN, 128), BF16),
            pltpu.VMEM((256, 256), BF16),
            pltpu.VMEM((3, 2, 80, 512), BF16),
            pltpu.VMEM((80, 512), BF16),
            pltpu.VMEM((80, 512), BF16),
            pltpu.VMEM((80, 512), BF16),
            pltpu.VMEM((4, 2, 2, 80, 512), BF16),
            pltpu.VMEM((2, 2, 80, 512), BF16),
            pltpu.VMEM((2, 2, 80, 1536), BF16),
            pltpu.VMEM((2, 2, 80, 512), BF16),
            pltpu.VMEM((4, 2, 2, 80, 512), BF16),
            pltpu.VMEM((2, 80, 512), BF16),
            pltpu.VMEM((2, 80, 512), BF16),
            pltpu.VMEM((2, 160, 2048), BF16),
            pltpu.VMEM((2, 2, 2, 80, 512), BF16),
            pltpu.VMEM((2, 4, 80, 512), BF16),
            pltpu.VMEM((2, 2, 144, 256), BF16),
            pltpu.VMEM((2, 2, 80, 256), BF16),
            pltpu.VMEM((2, 2, 80, 256), BF16),
            pltpu.VMEM((2, 2, 144, 256), BF16),
            pltpu.VMEM((2, 2, 80, 256), BF16),
            pltpu.VMEM((2, 2, 80, 256), BF16),
            dma((22,)),
            dma((6,)), dma((6,)),
            dma, dma,
            dma((2, 3)), dma((2, 4)),
            dma((10,)), dma((10,)),
        ],
        compiler_params=pltpu.CompilerParams(
            collective_id=0, has_side_effects=True, vmem_limit_bytes=62 * 2**20
        ),
        cost_estimate=pl.CostEstimate(flops=6_000_000_000, bytes_accessed=14_000_000, transcendentals=2_000_000),
    )(
        jnp.transpose(features, (0, 2, 1, 3)), packed_first, output_first, merge_weight, packed_second, output_second,
        pick, late, early, place,
        scale_first, row(gain_first), row(offset_first), row(merge_gain), row(merge_offset),
        scale_second, row(gain_second), row(offset_second),
        cut, keep, sides, heads,
    )
    return jnp.transpose(out.reshape(2, 12, 1, 12, 1024), (1, 2, 0, 3, 4))


def solution(mesh):
    return jax.shard_map(
        functools.partial(body, mesh.shape["lat"], mesh.shape["lon"]),
        mesh=mesh,
        in_specs=(P(None, "lat", "lon", None),) + (P(),) * 13,
        out_specs=P("lat", "lon", None, None, None),
        check_vma=False,
    )
```

```python
import functools

import jax
import jax.numpy as jnp
import numpy as np
from jax import lax
from jax.experimental import pallas as pl
from jax.experimental.pallas import tpu as pltpu
from jax.sharding import PartitionSpec as P

ATOM = 40
CELLS = 36
WIN = 4 * ATOM
MESH = pl.DeviceIdType.MESH
BF16 = jnp.bfloat16
F32 = jnp.float32
LOG2E = 1.4426950408889634
NORM_EPS = 1e-05
UNIT_EPS = 1e-06


def level_of(p, j):
    return (2 * p + j + 1) % 4


@functools.lru_cache(None)
def tables():
    cut = np.zeros((2, 160, 192), np.float32)
    for part in range(2):
        for hb in range(4):
            for i in range(3):
                for j in range(2):
                    for c in range(6):
                        row = hb * 40 + (i * 2 + j) * 6 + c
                        cut[part, row, (j * 6 + c) * 16 + 3 * hb + i + 4 * part] = 1
    pick = np.zeros((3, 160, 240), np.float32)
    for cp in range(2):
        for rp in range(2):
            for u in range(2):
                for i in range(3):
                    for j in range(2):
                        for c in range(3):
                            row = (cp * 2 + rp) * 40 + u * 18 + (i * 2 + j) * 3 + c
                            fine = 6 * u + 2 * i + rp
                            hb, at = 1 + fine // 3, (fine % 3 * 2 + j) * 6 + 2 * c + cp
                            pick[0, row, hb * 40 + at] = 1
                            for p in range(2):
                                pick[1 + p, row, (hb * 40 if hb < 4 else 160 + p * 40) + at] = 1
    late = np.zeros((320, 320), np.float32)
    early = np.zeros((288, 320), np.float32)
    for lane in range(4):
        for u in range(2):
            for j in range(2):
                for i in range(3):
                    for c in range(6):
                        src = lane * 80 + c // 3 * 40 + u * 18 + (i * 2 + j) * 3 + c % 3
                        late[(u * 2 + j) * 80 + lane * 18 + i * 6 + c, src] = 1
                        early[j * 144 + lane * 36 + u * 18 + i * 6 + c, src] = 1
    place = np.zeros((4, 144, 608), np.float32)
    for lane in range(4):
        for row in range(12):
            for col in range(12):
                half, c = (1, col) if col < 6 else (0, col - 6)
                if row < 3:
                    src = 448 + 80 * half + lane * 18 + row * 6 + c
                elif row < 9:
                    src = 144 * half + lane * 36 + (row - 3) * 6 + c
                else:
                    src = 288 + 80 * half + lane * 18 + (row - 9) * 6 + c
                place[lane, row * 12 + col, src] = 1
    t = np.arange(WIN) % ATOM
    atom = np.arange(WIN) // ATOM
    keep = np.stack(
        [
            (t // 6 % 2)[:, None] == (t // 6 % 2)[None],
            (atom % 2)[:, None] == (atom % 2)[None],
            (t % 18 // 3 % 2)[:, None] == (t % 18 // 3 % 2)[None],
            (t < 18)[:, None] == (t < 18)[None],
        ]
    ).astype(np.float32)
    valid = np.broadcast_to((t < CELLS)[:, None], (WIN, 128)).astype(np.float32)
    low = (np.arange(128) < 64)[None].astype(np.float32)
    sides = np.stack([valid * low, valid * (1 - low)])
    group = np.arange(256) // 64
    heads = (group[:, None] == group[None]).astype(np.float32)
    b = lambda x: x.astype(jnp.bfloat16)
    return b(cut), b(pick), b(late), b(early), b(place), b(keep), b(sides), b(heads)


def layer_norm(values, gain, offset):
    average = jnp.mean(values, axis=-1, keepdims=True)
    centred = values - average
    spread = jnp.mean(centred * centred, axis=-1, keepdims=True)
    return centred * lax.rsqrt(spread + NORM_EPS) * gain + offset


def dot(a, b):
    return jnp.dot(a, b, preferred_element_type=F32)


def head_scales(scale_ref):
    head = lax.broadcasted_iota(jnp.int32, (1, 512), 1) // 64
    factors = jnp.zeros((1, 512), F32)
    for h in range(8):
        factors = jnp.where(head == h, scale_ref[h] * LOG2E, factors)
    return factors


def project(x, weight_ref, heads_ref, factors, store):
    for at in range(3):
        y = dot(x, weight_ref[:, pl.ds(512 * at, 512)]).astype(BF16)
        if at < 2:
            squares = y * y
            total = jnp.concatenate(
                [dot(squares[:, :256], heads_ref[...]), dot(squares[:, 256:], heads_ref[...])], axis=1
            )
            inverse = lax.rsqrt(total + UNIT_EPS)
            y = (y.astype(F32) * (inverse * factors if at == 0 else inverse)).astype(BF16)
        store(512 * at, y)


def attend(fetch, store, mask, sides_ref):
    low = lax.broadcasted_iota(jnp.int32, (WIN, 128), 1) < 64
    for g in range(4):
        q, k, v = fetch(128 * g), fetch(512 + 128 * g), fetch(1024 + 128 * g)
        parts = []
        for side in range(2):
            key = k * sides_ref[side]
            value = v * sides_ref[side] + sides_ref[1 - side]
            score = lax.dot_general(q, key, (((1,), (1,)), ((), ())), preferred_element_type=F32)
            weight = jnp.exp2(score).astype(BF16)
            parts.append(dot(weight if mask is None else weight * mask, value))
        top = jnp.where(low, parts[0], parts[1])
        total = pltpu.roll(jnp.where(low, parts[1], parts[0]), 64, 1)
        store(128 * g, (top / total).astype(BF16))


def kernel(
    nlat, nlon,
    feat_hbm, packed1_hbm, out1_hbm, merge_hbm, packed2_hbm, out2_hbm,
    pick_hbm, late_hbm, early_hbm, place_hbm,
    scale1_hbm, gain1_hbm, offset1_hbm, gainm_hbm, offsetm_hbm, scale2_hbm, gain2_hbm, offset2_hbm,
    cut_hbm, keep_hbm, sides_hbm, heads_hbm,
    out,
    feat, packed1, wout1, wmerge, packed2, wout2, pick, late, early, place,
    scale1, gain1, offset1, gainm, offsetm, scale2, gain2, offset2, cut, keep, sides, heads,
    send0, send7, send_row, send_corner, x, rim, yn, ctx, first, edge_out, edge_in, picked, mb, quarter, t0, t1, t2, r0, r1, r2,
    load_sem, s1, v1, s2, v2, s3, v3, s4, v4,
):
    lat, lon = lax.axis_index("lat"), lax.axis_index("lon")
    odd = lax.rem(lon, 2)
    even = odd == 0

    def peer(dlat, dlon):
        return (lax.rem(lat + dlat + nlat, nlat), lax.rem(lon + dlon + nlon, nlon))

    def send(src, dst, send_sem, recv_sem, where):
        return pltpu.make_async_remote_copy(
            src_ref=src, dst_ref=dst, send_sem=send_sem, recv_sem=recv_sem,
            device_id=where, device_id_type=MESH,
        )

    def load(*pairs):
        copies = [pltpu.make_async_copy(a, b, load_sem.at[order.pop()]) for a, b in pairs]
        for copy in copies:
            copy.start()

        def wait():
            for copy in copies:
                copy.wait()

        return wait

    order = list(range(22))
    cut_loaded = load((feat_hbm, feat), (cut_hbm, cut))
    barrier = pltpu.get_barrier_semaphore()
    for dlat, dlon in [
        (0, 1), (0, -1), (0, -2), (1, 0), (1, 1), (-1, 0), (-1, -1), (-1, -2),
        (0, jnp.where(even, 2, -3)), (-1, jnp.where(even, 1, -3)),
    ]:
        pl.semaphore_signal(barrier, inc=1, device_id=peer(dlat, dlon), device_id_type=MESH)

    first_loaded = load(
        (packed1_hbm, packed1), (heads_hbm, heads), (keep_hbm, keep), (sides_hbm, sides), (scale1_hbm, scale1),
        (out1_hbm, wout1), (gain1_hbm, gain1), (offset1_hbm, offset1),
    )
    merge_loaded = load((pick_hbm, pick), (merge_hbm, wmerge), (gainm_hbm, gainm), (offsetm_hbm, offsetm))
    second_loaded = load(
        (packed2_hbm, packed2), (out2_hbm, wout2), (scale2_hbm, scale2), (gain2_hbm, gain2), (offset2_hbm, offset2),
        (late_hbm, late), (early_hbm, early), (place_hbm, place),
    )

    cut_loaded()

    feature_copies = [
        send(send0.at[n], x.at[n, 1], s1.at[n], v1.at[n], peer(0, -1)) for n in range(3)
    ] + [
        send(send7, rim.at[1, 0], s1.at[3], v1.at[3], peer(0, -1)),
        send(send_corner, rim.at[1, 1], s1.at[4], v1.at[4], peer(-1, -1)),
        send(send_row, rim.at[0, 1], s1.at[5], v1.at[5], peer(-1, 0)),
    ]

    def atoms_of(half, p, part):
        tokens = jnp.stack([
            feat[level_of(p, j), 6 * half : 6 * half + 6].astype(F32)[:, 8 * part : 8 * part + 16]
            for j in range(2)
        ]).astype(BF16).reshape(192, 512)
        return dot(cut[part], tokens).reshape(4, ATOM, 512)

    for half in range(2):
        upper = [atoms_of(half, p, 0) for p in range(2)]
        if half == 0:
            for p in range(2):
                send0[0, p] = upper[p][1:3].reshape(80, 512).astype(BF16)
            pl.semaphore_wait(barrier, jnp.where(even, 11, 9))
            feature_copies[0].start()
        lower = [atoms_of(half, p, 1) for p in range(2)]
        ends = [jnp.concatenate([a[n] for a in side], axis=0).astype(BF16) for side, n in ((upper, 0), (lower, 3))]
        for p in range(2):
            second = jnp.concatenate([upper[p][3], lower[p][0]], axis=0).astype(BF16)
            third = lower[p][1:3].reshape(80, 512).astype(BF16)
            if half == 0:
                send0[1, p] = second
                send0[2, p] = third
            else:
                x[0, 0, p] = upper[p][1:3].reshape(80, 512).astype(BF16)
                x[1, 0, p] = second
                x[2, 0, p] = third
        if half == 0:
            send7[...] = ends[1]
            send_corner[...] = ends[0]
            for copy in feature_copies[1:5]:
                copy.start()
        else:
            send_row[...] = ends[0]
            feature_copies[5].start()
            rim[0, 0] = ends[1]

    first_loaded()
    factors1 = head_scales(scale1)
    edge = send(edge_out, edge_in, s2, v2, peer(-1, 0))
    last_lat = lat == nlat - 1

    even_copies = [
        [
            send(mb.at[cb, 0, 0], quarter.at[cb, 3], s3.at[cb, 0], v3.at[cb, 3], peer(0, -2)),
            send(mb.at[cb, 0, 1], quarter.at[cb, 3], s3.at[cb, 1], v3.at[cb, 3], peer(0, -1)),
            send(mb.at[cb, 1, 1], quarter.at[cb, 0], s3.at[cb, 2], v3.at[cb, 0], peer(0, 1)),
        ]
        for cb in range(2)
    ]
    odd_copies = [
        [
            send(mb.at[cb, 0, 0], quarter.at[cb, 1], s3.at[cb, 0], v3.at[cb, 1], peer(0, -1)),
            send(mb.at[cb, 1, 0], quarter.at[cb, 2], s3.at[cb, 1], v3.at[cb, 2], peer(0, -1)),
        ]
        for cb in range(2)
    ]

    def merge(cb):
        for half in range(2):
            parts = []
            for p in range(2):
                if cb == 0:
                    moved = dot(pick[0], first[0:3, half, p].reshape(240, 512))
                else:
                    fine = jnp.concatenate([first[2:4, half, p].reshape(160, 512), edge_in[half]], axis=0)
                    moved = dot(pick[1 + p], fine)
                parts.append(moved.reshape(4, ATOM, 512))
            parts = jnp.concatenate(parts, axis=1).astype(BF16)
            for at in range(4):
                picked[cb, pl.ds(80 * half, 80), pl.ds(512 * at, 512)] = parts[at]
        normed = layer_norm(dot(picked[cb], wmerge[...]), gainm[...], offsetm[...])
        for half in range(2):
            for p in range(2):
                rows = normed[(half * 2 + p) * ATOM : (half * 2 + p + 1) * ATOM]
                mb[cb, half, p] = jnp.concatenate([rows[:, :512], rows[:, 512:]], axis=0).astype(BF16)

        @pl.when(even)
        def _():
            for copy in even_copies[cb]:
                copy.start()
            quarter[cb, 0] = mb[cb, 1, 0]

        @pl.when(jnp.logical_not(even))
        def _():
            for copy in odd_copies[cb]:
                copy.start()
            quarter[cb, 1] = mb[cb, 0, 1]
            quarter[cb, 2] = mb[cb, 1, 1]

    def merged_arrived(cb):
        @pl.when(even)
        def _():
            odd_copies[cb][0].wait_recv()
            odd_copies[cb][1].wait_recv()

        @pl.when(jnp.logical_not(even))
        def _():
            even_copies[cb][2].wait_recv()

        even_copies[cb][0].wait_recv()

    def band(b, carry):
        for n in range(3):
            @pl.when(b == n)
            def _():
                feature_copies[n].wait_recv()

        @pl.when(b == 3)
        def _():
            for n in range(3, 6):
                feature_copies[n].wait_recv()
            for half in range(2):
                near, far = rim[half, 0].astype(F32), rim[half, 1].astype(F32)
                for p in range(2):
                    rows = slice(ATOM * p, ATOM * p + ATOM)
                    x[3, half, p] = jnp.concatenate([near[rows], far[rows]], axis=0).astype(BF16)

        xb = x[b].reshape(320, 512)

        def keep_rows(at, y):
            yn[:, :, :, pl.ds(at, 512)] = y.reshape(2, 2, 80, 512)

        project(xb, packed1, heads, factors1, keep_rows)
        wrapped = jnp.where(jnp.logical_and(last_lat, b == 3), 1.0, 0.0).astype(F32)
        rows = keep[1].astype(F32) * wrapped + (1.0 - wrapped)
        for p in range(2):
            def fetch(at):
                return yn[:, p, :, pl.ds(at, 128)].reshape(WIN, 128)

            def keep_context(at, value):
                ctx[:, p, :, pl.ds(at, 128)] = value.reshape(2, 80, 128)

            mask = rows if p == 0 else rows * keep[0].astype(F32)
            attend(fetch, keep_context, mask.astype(BF16), sides)
        branch = layer_norm(dot(ctx[...].reshape(320, 512), wout1[...]), gain1[...], offset1[...])
        result = (xb.astype(F32) + branch).reshape(2, 2, 80, 512)
        first[b] = result.astype(BF16)

        @pl.when(b == 0)
        def _():
            edge_out[...] = result[:, :, :ATOM].reshape(2, 80, 512).astype(BF16)

        @pl.when(b == 1)
        def _():
            edge.start()

        @pl.when(b == 2)
        def _():
            merge_loaded()
            merge(0)
        return carry

    lax.fori_loop(0, 4, band, 0)

    edge.wait_recv()
    merge(1)

    second_loaded()
    factors2 = head_scales(scale2)
    odd_half = odd.astype(F32)
    levels = keep[2].astype(F32) * odd_half + (1.0 - odd_half)

    def keep_rows(at, y):
        yn[0, :, :, pl.ds(at, 512)] = y.reshape(2, 80, 512)

    def fetch(at):
        return yn[0, :, :, pl.ds(at, 128)].reshape(WIN, 128)

    def keep_context(at, value):
        ctx[0, :, :, pl.ds(at, 128)] = value.reshape(2, 80, 128)

    final_copies = []
    for cb in range(2):
        merged_arrived(cb)
        if cb == 1:
            wrapped = jnp.where(last_lat, 1.0, 0.0).astype(F32)
            mask = levels * (keep[3].astype(F32) * wrapped + (1.0 - wrapped))
        else:
            mask = levels
        own = [quarter[cb, n].astype(F32) for n in range(4)]
        own = jnp.concatenate([jnp.concatenate([q[:ATOM], q[ATOM:]], axis=1) for q in own], axis=0)
        project(own.astype(BF16), packed2, heads, factors2, keep_rows)
        attend(fetch, keep_context, mask.astype(BF16), sides)
        for half in (1, 0):
            branch = layer_norm(dot(ctx[0, half], wout2[...]), gain2[...], offset2[...])
            second = (own[80 * half : 80 * half + 80] + branch).astype(BF16)
            stacked = jnp.concatenate([second[:, 256 * n : 256 * n + 256] for n in range(4)], axis=0)
            if cb == 1:
                units = dot(late[...], stacked).astype(BF16).reshape(2, 2, 80, 256)
                if half == 0:
                    r1[0, 0] = units[0, 0]
                t1[half] = units[0]
                t2[half] = units[1]
            else:
                units = dot(early[...], stacked).astype(BF16).reshape(2, 144, 256)
                if half == 0:
                    r0[0, 0] = units[0]
                t0[half] = units
            for j in range(2):
                to = 2 * half + (0 if j == 0 else 1 - 2 * odd)
                n = half * 2 + j
                if cb == 1:
                    final_copies.append(
                        send(t2.at[half, j], r2.at[half, j], s4.at[n], v4.at[n], peer(1, to)))
                    final_copies[-1].start()
                if n > 0:
                    src, dst, base = (t1, r1, 3) if cb == 1 else (t0, r0, 6)
                    final_copies.append(
                        send(src.at[half, j], dst.at[half, j], s4.at[base + n], v4.at[base + n], peer(0, to)))
                    final_copies[-1].start()

    for copy in final_copies:
        copy.wait_recv()
    for level in range(2):
        j = 1 - level
        parts = [r[half, j] for r in (r0, r1, r2) for half in range(2)]
        parts = jnp.concatenate(parts, axis=0)
        for n in range(4):
            out[level, :, pl.ds(256 * n, 256)] = dot(place[n], parts).astype(BF16)

    for copy in feature_copies:
        copy.wait_send()
    edge.wait_send()

    @pl.when(even)
    def _():
        for copy in even_copies[0] + even_copies[1]:
            copy.wait_send()

    @pl.when(jnp.logical_not(even))
    def _():
        for copy in odd_copies[0] + odd_copies[1]:
            copy.wait_send()

    for copy in final_copies:
        copy.wait_send()


def body(nlat, nlon, features, packed_first, scale_first, output_first, gain_first, offset_first,
         merge_weight, merge_gain, merge_offset,
         packed_second, scale_second, output_second, gain_second, offset_second):
    any_spec = pl.BlockSpec(memory_space=pl.ANY)
    vmem = pl.BlockSpec(memory_space=pltpu.VMEM)
    dma = pltpu.SemaphoreType.DMA
    row = lambda v: v.reshape(1, -1)
    *small, keep, sides, heads = [jnp.asarray(t) for t in tables()]
    cut, pick, late, early, place = small
    out = pl.pallas_call(
        functools.partial(kernel, nlat, nlon),
        out_shape=jax.ShapeDtypeStruct((2, 144, 1024), BF16),
        in_specs=[any_spec] * 22,
        out_specs=vmem,
        scratch_shapes=[
            pltpu.VMEM((4, 12, 24, 512), BF16),
            pltpu.VMEM((512, 1536), BF16),
            pltpu.VMEM((512, 512), BF16),
            pltpu.VMEM((2048, 1024), BF16),
            pltpu.VMEM((1024, 1536), BF16),
            pltpu.VMEM((512, 1024), BF16),
            pltpu.VMEM((3, 160, 240), BF16),
            pltpu.VMEM((320, 320), BF16),
            pltpu.VMEM((288, 320), BF16),
            pltpu.VMEM((4, 144, 608), BF16),
            pltpu.SMEM((8,), F32),
            *[pltpu.VMEM((1, 512), F32)] * 2,
            *[pltpu.VMEM((1, 1024), F32)] * 2,
            pltpu.SMEM((8,), F32),
            *[pltpu.VMEM((1, 1024), F32)] * 2,
            pltpu.VMEM((2, 160, 192), BF16),
            pltpu.VMEM((4, WIN, WIN), BF16),
            pltpu.VMEM((2, WIN, 128), BF16),
            pltpu.VMEM((256, 256), BF16),
            pltpu.VMEM((3, 2, 80, 512), BF16),
            pltpu.VMEM((80, 512), BF16),
            pltpu.VMEM((80, 512), BF16),
            pltpu.VMEM((80, 512), BF16),
            pltpu.VMEM((4, 2, 2, 80, 512), BF16),
            pltpu.VMEM((2, 2, 80, 512), BF16),
            pltpu.VMEM((2, 2, 80, 1536), BF16),
            pltpu.VMEM((2, 2, 80, 512), BF16),
            pltpu.VMEM((4, 2, 2, 80, 512), BF16),
            pltpu.VMEM((2, 80, 512), BF16),
            pltpu.VMEM((2, 80, 512), BF16),
            pltpu.VMEM((2, 160, 2048), BF16),
            pltpu.VMEM((2, 2, 2, 80, 512), BF16),
            pltpu.VMEM((2, 4, 80, 512), BF16),
            pltpu.VMEM((2, 2, 144, 256), BF16),
            pltpu.VMEM((2, 2, 80, 256), BF16),
            pltpu.VMEM((2, 2, 80, 256), BF16),
            pltpu.VMEM((2, 2, 144, 256), BF16),
            pltpu.VMEM((2, 2, 80, 256), BF16),
            pltpu.VMEM((2, 2, 80, 256), BF16),
            dma((22,)),
            dma((6,)), dma((6,)),
            dma, dma,
            dma((2, 3)), dma((2, 4)),
            dma((10,)), dma((10,)),
        ],
        compiler_params=pltpu.CompilerParams(
            collective_id=0, has_side_effects=True, vmem_limit_bytes=62 * 2**20
        ),
        cost_estimate=pl.CostEstimate(flops=6_000_000_000, bytes_accessed=14_000_000, transcendentals=2_000_000),
    )(
        jnp.transpose(features, (0, 2, 1, 3)), packed_first, output_first, merge_weight, packed_second, output_second,
        pick, late, early, place,
        scale_first, row(gain_first), row(offset_first), row(merge_gain), row(merge_offset),
        scale_second, row(gain_second), row(offset_second),
        cut, keep, sides, heads,
    )
    return jnp.transpose(out.reshape(2, 12, 1, 12, 1024), (1, 2, 0, 3, 4))


def solution(mesh):
    return jax.shard_map(
        functools.partial(body, mesh.shape["lat"], mesh.shape["lon"]),
        mesh=mesh,
        in_specs=(P(None, "lat", "lon", None),) + (P(),) * 13,
        out_specs=P("lat", "lon", None, None, None),
        check_vma=False,
    )
```
